256 devices in a mesh: dp: 4 (over y), seq: 64 (over z, x, core).
Axes of the slice: x: 4, y: 4, z: 8, core: 2. Of those that a mesh axis runs over, the one named last changes fastest.
Arguments:
- query_rows: bfloat16 [4, 16384, 2048], P('dp', 'seq'), may hold values from -12 to 12
- key_rows: bfloat16 [4, 16384, 2048], P('dp', 'seq'), may hold values from -12 to 12
- value_rows: bfloat16 [4, 16384, 2048], P('dp', 'seq'), may hold values from -6 to 6
- output_grad: bfloat16 [4, 16384, 2048], P('dp', 'seq'), may hold values from -6 to 6
- query_gain: float32 [16, 128], replicated, may hold values from 0.5 to 6
- key_gain: float32 [16, 128], replicated, may hold values from 0.5 to 6
- block_list: int32 [4, 16, 128, 8], P('dp'), may hold values from 0 to 127, as said below
- block_count: int32 [4, 16, 128], P('dp'), may hold values from 1 to 8, as said below
Outputs:
- attended: bfloat16 [4, 16384, 2048], P('dp', 'seq')
- query_grad: bfloat16 [4, 16384, 2048], P('dp', 'seq')
- key_grad: bfloat16 [4, 16384, 2048], P('dp', 'seq')
- value_grad: bfloat16 [4, 16384, 2048], P('dp', 'seq')
- query_gain_grad: float32 [16, 128], replicated
- key_gain_grad: float32 [16, 128], replicated
The draws below stay inside these ranges and needn't reach their ends.
Inputs may be any that keep to these rules, and one draw needn't show every extreme that they name: `block_list`: for every sample, head and query block the 8 entries are distinct block numbers, and the first is the query block itself. Only the first block_count entries of a list are used. In every sample and head some query block uses all 8.
All inputs are finite; a program needn't handle non-finite values.
Results may differ from the reference program's by a relative error of at most 0.03.
The reference program's roundings to bfloat16 on the way count: a program that leaves them out, or rounds other values in their place, can miss the bound.
Values may be sent and summed in bfloat16 or wider, within the bound.
No kernel may reach another device: no remote copies, remote signals or barrier semaphores. Data moves between devices by JAX's collectives and lax.ppermute only.
A program may use at most 128 MiB of HBM per device.

```python
import math
import jax
import jax.numpy as jnp
from jax import lax

HEADS = 16
HEAD_DIM = 128
BLOCK = 128
MOST = 8
TOK_DEV = 256
D = 2048
SAMPLES = 4
SEQ_LEN = 16384
SAMPLE_BLOCKS = 128
SETS = 4
SET_ROWS = 64


def spread_rows(base_key):
    noise_draw = jnp.clip(jax.random.normal(base_key, (SAMPLES, SEQ_LEN, D), jnp.float32), -3.0, 3.0)
    levels = jax.random.uniform(jax.random.fold_in(base_key, 1), (SAMPLES, SEQ_LEN, 1), jnp.float32, math.log(0.5), math.log(5.0))
    return noise_draw * jnp.exp(levels)


def draw_key_rows(key, part):
    common = spread_rows(key)
    return jnp.clip(common, -12.0, 12.0).astype(jnp.bfloat16)


def draw_query_rows(key, part):
    key = jax.random.fold_in(key, 5)
    fresh_rows = spread_rows(key)
    return jnp.clip(fresh_rows, -12.0, 12.0).astype(jnp.float32).astype(jnp.bfloat16)


def gain_draw(gain_key):
    return jnp.exp(jax.random.uniform(gain_key, (HEADS, HEAD_DIM), jnp.float32, math.log(0.5), math.log(2.0)))


def draw_query_gain(key, part):
    key = jax.random.fold_in(key, 7)
    return gain_draw(key)


def draw_key_gain(key, part):
    key = jax.random.fold_in(key, 9)
    return gain_draw(key)


def draw_block_list(key, part):
    key = jax.random.fold_in(key, 13)
    ranking_sample = jax.random.randint(key, (SAMPLES, HEADS, SAMPLE_BLOCKS, SAMPLE_BLOCKS), 0, 1 << 16)
    block_numbers = jnp.arange(SAMPLE_BLOCKS, dtype=jnp.int32)
    block_distance = jnp.abs(block_numbers[:, None] - block_numbers[None, :])
    nearby_reward = jnp.where(block_distance == 0, 1 << 18, jnp.where(block_distance <= 2, 1 << 16, 0))
    block_ordering = (ranking_sample + nearby_reward[None, None]) * SAMPLE_BLOCKS + block_numbers[None, None, None, :]
    return lax.top_k(block_ordering, MOST)[1].astype(jnp.int32)


def draw_block_count(key, part):
    key = jax.random.fold_in(key, 17)
    shift_draw = jax.random.randint(key, (SAMPLES, HEADS, 1), 0, 4)
    cap_draw = jnp.maximum(1, MOST // jnp.left_shift(1, shift_draw))
    count_draw = 1 + jax.random.randint(jax.random.fold_in(key, 1), (SAMPLES, HEADS, SAMPLE_BLOCKS), 0, 1 << 20) % cap_draw
    full_at = jax.random.randint(jax.random.fold_in(key, 2), (SAMPLES, HEADS, 1), 0, SAMPLE_BLOCKS)
    block_numbers = jnp.arange(SAMPLE_BLOCKS, dtype=jnp.int32)
    return jnp.where(block_numbers[None, None, :] == full_at, MOST, count_draw).astype(jnp.int32)


def level_of(own_key, shape, cuts, least, high):
    level = 1.0
    for dim, blocks in cuts:
        steps = jax.random.uniform(jax.random.fold_in(jax.random.fold_in(own_key, 6), dim), (blocks,), jnp.float32, least / len(cuts), high / len(cuts))
        level = level * jnp.repeat(jnp.exp(steps), shape[dim] // blocks).reshape((-1,) + (1,) * (len(shape) - 1 - dim))
    return level


def normal_values(own_key, shape, scale, limit, pieces=(), kind=jnp.bfloat16):
    factor_of = level_of(own_key, shape, pieces, -0.22, 0.18) if pieces else 1.0
    drawn = jax.random.normal(own_key, shape, jnp.float32) * scale * factor_of
    return jnp.minimum(jnp.maximum(drawn, -limit), limit).astype(kind)


def setup_inputs(seed: int = 0) -> dict:
    key_list = jax.random.split(jax.random.key(seed), 9)
    query_rows = draw_query_rows(jax.random.fold_in(key_list[8], 71), 0)
    key_rows = draw_key_rows(jax.random.fold_in(key_list[8], 71), 0)
    value_rows = normal_values(key_list[2], (SAMPLES, SEQ_LEN, D), 1.0, 6.0, ((0, 4), (1, 64)))
    output_grad = normal_values(key_list[3], (SAMPLES, SEQ_LEN, D), 1.0, 6.0, ((0, 4), (1, 64)))
    query_gain = draw_query_gain(jax.random.fold_in(key_list[8], 71), 0)
    key_gain = draw_key_gain(jax.random.fold_in(key_list[8], 71), 0)
    block_list = draw_block_list(jax.random.fold_in(key_list[8], 71), 0)
    block_count = draw_block_count(jax.random.fold_in(key_list[8], 71), 0)
    return dict(query_rows=query_rows, key_rows=key_rows, value_rows=value_rows, output_grad=output_grad, query_gain=query_gain, key_gain=key_gain, block_list=block_list, block_count=block_count)


EPS = 1e-06

def inverse_root(wide_rows):
    return lax.rsqrt(lax.optimization_barrier(jnp.mean(wide_rows * wide_rows, axis=-1, keepdims=True)) + EPS)

def norm_backward(wide_rows, row_scale, gain_row, upstream_grad):
    weighted = upstream_grad * gain_row
    inner_mean = lax.optimization_barrier(jnp.mean(weighted * wide_rows, axis=-1, keepdims=True))
    return row_scale * weighted - wide_rows * (row_scale * row_scale * row_scale) * inner_mean

def one_head(query_col, key_col, value_col, grad_col, gain_query, gain_key, list_table, count_table):
    inv_root = 1.0 / math.sqrt(HEAD_DIM)
    query_wide = query_col.astype(jnp.float32)
    query_scale = inverse_root(query_wide)
    query_hat = query_wide * query_scale
    query_norm = (query_hat * gain_query).astype(jnp.bfloat16)
    key_broadened = key_col.astype(jnp.float32)
    key_scale = inverse_root(key_broadened)
    key_hat = key_broadened * key_scale
    key_norm = (key_hat * gain_key).astype(jnp.bfloat16)
    key_blocks = key_norm.reshape(SAMPLE_BLOCKS, BLOCK, HEAD_DIM)
    value_blocks = value_col.reshape(SAMPLE_BLOCKS, BLOCK, HEAD_DIM)
    group_rows = math.gcd(SET_ROWS, BLOCK)
    group_total = SEQ_LEN // group_rows
    per_step = math.gcd(group_total, max(1, 512 // group_rows))
    step_total = group_total // per_step
    key_span = MOST * BLOCK

    def step(carry, step_index):
        key_acc, value_acc, gain_acc = carry
        starts = (step_index * per_step + jnp.arange(per_step, dtype=jnp.int32)) * group_rows
        block_numbers = (starts // BLOCK).astype(jnp.int32)
        set_ids = (starts % TOK_DEV // SET_ROWS).astype(jnp.int32)
        picked = list_table[block_numbers]
        live_count = count_table[block_numbers]
        row_ids = (starts[:, None] + jnp.arange(group_rows, dtype=jnp.int32)[None, :]).astype(jnp.int32)
        query_pick = query_norm[row_ids].astype(jnp.float32)
        hat_pick = query_hat[row_ids]
        wide_pick = query_wide[row_ids]
        scale_pick = query_scale[row_ids]
        grad_pick = grad_col[row_ids].astype(jnp.float32)
        key_pick = key_blocks[picked].reshape(per_step, key_span, HEAD_DIM).astype(jnp.float32)
        value_pick = value_blocks[picked].reshape(per_step, key_span, HEAD_DIM).astype(jnp.float32)
        live_mask = jnp.repeat(jnp.arange(MOST, dtype=jnp.int32)[None, :] < live_count[:, None], BLOCK, axis=1)
        scores = jnp.einsum('gqe,gke->gqk', query_pick, key_pick) * inv_root
        scores = jnp.where(live_mask[:, None, :], scores, -jnp.inf)
        row_max = lax.optimization_barrier(jnp.max(scores, axis=-1, keepdims=True))
        exp_scores = jnp.exp(scores - row_max)
        weights = (exp_scores / lax.optimization_barrier(jnp.sum(exp_scores, axis=-1, keepdims=True))).astype(jnp.bfloat16)
        weights_wide = weights.astype(jnp.float32)
        attended = jnp.einsum('gqk,gke->gqe', weights_wide, value_pick).astype(jnp.bfloat16)
        weight_grad = jnp.einsum('gqe,gke->gqk', grad_pick, value_pick)
        row_inner = lax.optimization_barrier(jnp.sum(grad_pick * attended.astype(jnp.float32), axis=-1, keepdims=True))
        score_grad = (weights_wide * (weight_grad - row_inner)).astype(jnp.bfloat16).astype(jnp.float32)
        norm_grad = jnp.einsum('gqk,gke->gqe', score_grad, key_pick) * inv_root
        key_term = jnp.einsum('gqk,gqe->gke', score_grad, query_pick) * inv_root
        value_term = jnp.einsum('gqk,gqe->gke', weights_wide, grad_pick)
        key_acc = key_acc.at[set_ids[:, None], picked].add(key_term.reshape(per_step, MOST, BLOCK, HEAD_DIM))
        value_acc = value_acc.at[set_ids[:, None], picked].add(value_term.reshape(per_step, MOST, BLOCK, HEAD_DIM))
        gain_acc = gain_acc + lax.optimization_barrier(jnp.sum(norm_grad * hat_pick, axis=(0, 1)))
        query_grad = norm_backward(wide_pick, scale_pick, gain_query, norm_grad).astype(jnp.bfloat16)
        return ((key_acc, value_acc, gain_acc), (attended, query_grad))
    start_carry = (jnp.zeros((SETS, SAMPLE_BLOCKS, BLOCK, HEAD_DIM), jnp.float32), jnp.zeros((SETS, SAMPLE_BLOCKS, BLOCK, HEAD_DIM), jnp.float32), jnp.zeros((HEAD_DIM,), jnp.float32))
    final_carry, outputs = lax.scan(step, start_carry, jnp.arange(step_total, dtype=jnp.int32))
    key_acc, value_acc, query_gain_part = final_carry
    attended = outputs[0].reshape(SEQ_LEN, HEAD_DIM)
    query_grad = outputs[1].reshape(SEQ_LEN, HEAD_DIM)
    key_round = lax.optimization_barrier(key_acc.astype(jnp.bfloat16))
    value_round = lax.optimization_barrier(value_acc.astype(jnp.bfloat16))
    key_total = lax.optimization_barrier(jnp.sum(key_round.astype(jnp.float32), axis=0)).reshape(SEQ_LEN, HEAD_DIM)
    value_grad = lax.optimization_barrier(jnp.sum(value_round.astype(jnp.float32), axis=0)).astype(jnp.bfloat16).reshape(SEQ_LEN, HEAD_DIM)
    key_grad = norm_backward(key_broadened, key_scale, gain_key, key_total).astype(jnp.bfloat16)
    key_gain_part = lax.optimization_barrier(jnp.sum(key_total * key_hat, axis=0))
    return (attended, query_grad, key_grad, value_grad, query_gain_part, key_gain_part)

def by_head(array):
    return jnp.transpose(array.reshape(SEQ_LEN, HEADS, HEAD_DIM), (1, 0, 2))

def merge_heads(array):
    return jnp.transpose(array, (1, 0, 2)).reshape(SEQ_LEN, HEADS * HEAD_DIM)

def head_call(head_items):
    return one_head(head_items[0], head_items[1], head_items[2], head_items[3], head_items[4], head_items[5], head_items[6], head_items[7])

def reference(query_rows, key_rows, value_rows, output_grad, query_gain, key_gain, block_list, block_count):

    def per_sample(sample_items):
        query_one, key_one, value_one, grad_one, lists_one, counts_one = sample_items
        results = lax.map(head_call, (by_head(query_one), by_head(key_one), by_head(value_one), by_head(grad_one), query_gain, key_gain, lists_one, counts_one))
        return (merge_heads(results[0]), merge_heads(results[1]), merge_heads(results[2]), merge_heads(results[3]), results[4], results[5])
    outputs = lax.map(per_sample, (query_rows, key_rows, value_rows, output_grad, block_list, block_count))
    return (outputs[0], outputs[1], outputs[2], outputs[3], lax.optimization_barrier(jnp.sum(outputs[4], axis=0)), lax.optimization_barrier(jnp.sum(outputs[5], axis=0)))
```

```python
import functools, math
import jax
import jax.numpy as jnp
from jax import lax
from jax.experimental import pallas as pl
from jax.experimental.pallas import tpu as pltpu
from jax.sharding import PartitionSpec as P

HEAD_DIM = 128
EPS = 1e-06
INV_ROOT = 1.0 / math.sqrt(HEAD_DIM)
NT = (((1,), (1,)), ((), ()))
TN = (((0,), (0,)), ((), ()))
NN = (((1,), (0,)), ((), ()))


def dot(a, b, dims):
    return lax.dot_general(a, b, dims, preferred_element_type=jnp.float32)


def attend_kernel(order_ref, count_ref, list_ref, bound_ref, kv0, kv1, kv2, kv3, qg_ref, gains_ref,
                  og_ref, p0, p1, p2, p3, gain_ref, ktab, vtab, acck, accv, sems, *, per_step, buckets):
    pieces = (kv0, kv1, kv2, kv3)
    copies = []
    for i, piece in enumerate(pieces):
        where = pl.ds((i % 2) * 64, 64)
        rows = pl.ds((i // 2) * 64, 64)
        for j, table in enumerate((ktab, vtab)):
            copies.append(pltpu.make_async_copy(piece.at[:, j], table.at[where, rows], sems.at[2 * i + j]))
    for copy in copies:
        copy.start()

    @pl.loop(0, 128)
    def _(t):
        acck[t] = jnp.zeros((128, 128), jnp.float32)
        accv[t] = jnp.zeros((128, 128), jnp.float32)

    gain_query = gains_ref[0:1, :]
    gain_key = gains_ref[1:2, :]
    gain_ref[...] = jnp.zeros_like(gain_ref)
    for copy in copies:
        copy.wait()

    @pl.loop(0, 128, unroll=2)
    def _(t):
        wide = ktab[t].astype(jnp.float32)
        scale = lax.rsqrt(jnp.mean(wide * wide, axis=-1, keepdims=True) + EPS)
        ktab[t] = (wide * scale * gain_key).astype(jnp.bfloat16)

    def one_group(i, most):
        g = order_ref[i]
        live = count_ref[i]
        spots = [list_ref[i * 8 + j] for j in range(most)]
        wide = qg_ref[g, 0].astype(jnp.float32)
        grad = qg_ref[g, 1]
        scale = lax.rsqrt(jnp.mean(wide * wide, axis=-1, keepdims=True) + EPS)
        hat = wide * scale
        normed = (hat * gain_query).astype(jnp.bfloat16)
        keys = [ktab[t] for t in spots]
        values = [vtab[t] for t in spots]
        scores = []
        for j in range(most):
            s = dot(normed, keys[j], NT) * INV_ROOT
            if j:
                s = jnp.where(j < live, s, -jnp.inf)
            scores.append(s)
        top = jnp.max(functools.reduce(jnp.maximum, scores), axis=-1, keepdims=True)
        exps = [jnp.exp(s - top) for s in scores]
        total = jnp.sum(functools.reduce(jnp.add, exps), axis=-1, keepdims=True)
        inverse = 1.0 / total
        weights = [(e * inverse).astype(jnp.bfloat16) for e in exps]
        attended = functools.reduce(jnp.add, [dot(w, v, NN) for w, v in zip(weights, values)]).astype(jnp.bfloat16)
        og_ref[g, 0] = attended
        inner = jnp.sum(grad.astype(jnp.float32) * attended.astype(jnp.float32), axis=-1, keepdims=True)
        score_grads = []
        for j in range(most):
            wg = dot(grad, values[j], NT)
            score_grads.append((weights[j].astype(jnp.float32) * (wg - inner)).astype(jnp.bfloat16))
        norm_grad = functools.reduce(jnp.add, [dot(s, k, NN) for s, k in zip(score_grads, keys)]) * INV_ROOT
        for j in range(most):
            acck[spots[j]] += dot(score_grads[j], normed, TN)
            accv[spots[j]] += dot(weights[j], grad, TN)
        gain_ref[0:1, :] += jnp.sum(norm_grad * hat, axis=0, keepdims=True)
        weighted = norm_grad * gain_query
        mean = jnp.mean(weighted * wide, axis=-1, keepdims=True)
        og_ref[g, 1] = (scale * weighted - wide * (scale * scale * scale) * mean).astype(jnp.bfloat16)

    start = 0
    for which, most in enumerate(buckets):
        stop = bound_ref[which]

        @pl.loop(start, stop)
        def _(step, most=most):
            for u in range(per_step):
                one_group(step * per_step + u, most)

        start = stop

    outs = (p0, p1, p2, p3)

    @pl.loop(0, 64)
    def _(s):
        for x in range(2):
            k = acck[x * 64 + s] * INV_ROOT
            v = accv[x * 64 + s]
            for c in range(2):
                outs[2 * c + x][s, 0] = k[c * 64:(c + 1) * 64].astype(jnp.bfloat16)
                outs[2 * c + x][s, 1] = v[c * 64:(c + 1) * 64].astype(jnp.bfloat16)


def attend(order, counts, lists, bounds, kv0, kv1, kv2, kv3, qg, gains, per_step=2, buckets=(8, 6, 4, 2)):
    smem = pl.BlockSpec(memory_space=pltpu.SMEM)
    vmem = pl.BlockSpec(memory_space=pltpu.VMEM)
    hbm = pl.BlockSpec(memory_space=pl.ANY)
    piece = jax.ShapeDtypeStruct((64, 2, 64, 128), jnp.bfloat16)
    return pl.pallas_call(
        functools.partial(attend_kernel, per_step=per_step, buckets=buckets),
        out_shape=(piece, piece, piece, piece, piece, jax.ShapeDtypeStruct((8, 128), jnp.float32)),
        in_specs=[smem] * 4 + [hbm] * 4 + [vmem] * 2,
        out_specs=(vmem,) * 6,
        scratch_shapes=[
            pltpu.VMEM((128, 128, 128), jnp.bfloat16),
            pltpu.VMEM((128, 128, 128), jnp.bfloat16),
            pltpu.VMEM((128, 128, 128), jnp.float32),
            pltpu.VMEM((128, 128, 128), jnp.float32),
            pltpu.SemaphoreType.DMA((8,)),
        ],
        compiler_params=pltpu.CompilerParams(vmem_limit_bytes=56 * 1024 * 1024),
    )(order, counts, lists, bounds, kv0, kv1, kv2, kv3, qg, gains)


def sorted_tables(counts, lists, per_step, buckets):
    index = jnp.arange(64, dtype=jnp.int32)
    ahead = (counts[None, :] > counts[:, None]) | ((counts[None, :] == counts[:, None]) & (index[None, :] < index[:, None]))
    rank = jnp.sum(ahead.astype(jnp.int32), axis=1)
    place = (rank[None, :] == index[:, None]).astype(jnp.int32)
    order = jnp.sum(place * index[None, :], axis=1)
    sorted_counts = jnp.sum(place * counts[None, :], axis=1)
    sorted_lists = jnp.sum(place[:, :, None] * lists[None, :, :], axis=1)
    bounds = [(jnp.sum((counts > b).astype(jnp.int32)) + per_step - 1) // per_step for b in buckets[1:]]
    bounds = jnp.stack(bounds + [jnp.int32(64 // per_step)])
    return order, sorted_counts, sorted_lists.reshape(-1), bounds


HEADS = 16
MOST = 8
PER_STEP = 2
BUCKETS = (8, 6, 4, 2)


def to_send(rows):
    return jnp.transpose(rows.reshape(4, 64, HEADS, HEAD_DIM), (2, 0, 1, 3)).reshape(64, 64, HEAD_DIM)


def from_back(pieces):
    return jnp.transpose(pieces.reshape(HEADS, 4, 64, HEAD_DIM), (1, 2, 0, 3)).reshape(1, 256, HEADS * HEAD_DIM)


def exchange(array):
    return lax.all_to_all(array, "seq", split_axis=0, concat_axis=0, tiled=True)


def across(array, flip):
    return lax.ppermute(array, "seq", [(i, i ^ flip) for i in range(64)])


def body(query_rows, key_rows, value_rows, output_grad, query_gain, key_gain, block_list, block_count):
    position = lax.axis_index("seq")
    head = position // 4
    chip = position // 2 % 2
    lists = lax.dynamic_slice_in_dim(block_list[0], head, 1, 0).reshape(64, 2, MOST)
    counts = lax.dynamic_slice_in_dim(block_count[0], head, 1, 0).reshape(64, 2)
    lists = jnp.where(chip == 0, lists[:, 0], lists[:, 1])
    counts = jnp.where(chip == 0, counts[:, 0], counts[:, 1])
    lists = (lists % 2 ^ chip) * 64 + lists // 2
    order, counts, lists, bounds = sorted_tables(counts, lists, PER_STEP, BUCKETS)
    gain_query = lax.dynamic_slice_in_dim(query_gain, head, 1, 0)
    gain_key = lax.dynamic_slice_in_dim(key_gain, head, 1, 0)
    gains = jnp.concatenate([gain_query, gain_key], axis=0)

    with jax.named_scope("gather"):
        kv_own = exchange(jnp.stack([to_send(key_rows[0]), to_send(value_rows[0])], axis=1))
        query_rows, output_grad, kv_own = lax.optimization_barrier((query_rows, output_grad, kv_own))
        kv_chip = across(kv_own, 2)
        query_grad_pair = exchange(jnp.stack([to_send(query_rows[0]), to_send(output_grad[0])], axis=1))
        kv_core = across(kv_own, 1)
        kv_far = across(kv_chip, 1)
    with jax.named_scope("attend"):
        outs = attend(order, counts, lists, bounds, kv_own, kv_chip, kv_core, kv_far, query_grad_pair, gains, PER_STEP, BUCKETS)
    front, part_own, part_chip, part_core, part_far, query_gain_rows = outs
    with jax.named_scope("return"):
        far = part_chip.astype(jnp.float32) + across(part_far, 1).astype(jnp.float32)
        far = across(far.astype(jnp.bfloat16), 2)
        front_back = exchange(front)
        near = part_own.astype(jnp.float32) + across(part_core, 1).astype(jnp.float32)
        total = near + far.astype(jnp.float32)
        key_total, value_total = total[:, 0], total[:, 1]
        wide = kv_own[:, 0].astype(jnp.float32)
        scale = lax.rsqrt(jnp.mean(wide * wide, axis=-1, keepdims=True) + EPS)
        weighted = key_total * gain_key
        inner = jnp.mean(weighted * wide, axis=-1, keepdims=True)
        key_grad = scale * weighted - wide * (scale * scale * scale) * inner
        key_gain_row = jnp.sum(key_total * (wide * scale), axis=(0, 1))
        back = exchange(jnp.stack([key_grad, value_total], axis=1).astype(jnp.bfloat16))
    with jax.named_scope("gains"):
        mine = jnp.stack([query_gain_rows[0], key_gain_row])
        for flip in (1, 2):
            mine = mine + lax.ppermute(mine, "dp", [(i, i ^ flip) for i in range(4)])
        for flip in (1, 2):
            mine = mine + across(mine, flip)
        gathered = mine[None]
        for step, flip in enumerate((4, 8, 16, 32)):
            other = across(gathered, flip)
            low = (position // flip) % 2 == 0
            gathered = jnp.where(low, jnp.concatenate([gathered, other]), jnp.concatenate([other, gathered]))
    return (
        from_back(front_back[:, 0]),
        from_back(front_back[:, 1]),
        from_back(back[:, 0]),
        from_back(back[:, 1]),
        gathered[:, 0],
        gathered[:, 1],
    )


def solution(mesh):
    rows = P("dp", "seq", None)
    return jax.shard_map(
        body,
        mesh=mesh,
        in_specs=(rows, rows, rows, rows, P(), P(), P("dp", None, None, None), P("dp", None, None)),
        out_specs=(rows, rows, rows, rows, P(), P()),
        check_vma=False,
    )
```

```python
import functools
import math

import jax
import jax.numpy as jnp
from jax import lax
from jax.experimental import pallas as pl
from jax.experimental.pallas import tpu as pltpu
from jax.sharding import PartitionSpec as P

HEAD_DIM = 128
EPS = 1e-06
INV_ROOT = 1.0 / math.sqrt(HEAD_DIM)
LOG2E = math.log2(math.e)
NT = (((1,), (1,)), ((), ()))
TN = (((0,), (0,)), ((), ()))
NN = (((1,), (0,)), ((), ()))
GROUPS = 32
BUCKETS = (8, 6, 4, 2)
TOGETHER = 1


def dot(a, b, dims):
    return lax.dot_general(a, b, dims, preferred_element_type=jnp.float32)


def attend_kernel(info_ref, count_ref, list_ref, k0, k1, k2, k3, v0, v1, v2, v3, qg_hbm, gains_ref,
                  og_hbm, p0, p1, p2, p3, gain_ref,
                  ktab, vtab, acc, qg_ref, og_ref, stage, order_ref, in_sems, out_sems):
    mine = info_ref[0]
    chip = info_ref[1]
    copies = [pltpu.make_async_copy(qg_hbm, qg_ref, in_sems.at[8])]
    for j, (pieces, table) in enumerate((((k0, k1, k2, k3), ktab), ((v0, v1, v2, v3), vtab))):
        for i, piece in enumerate(pieces):
            to = table.at[pl.ds((i % 2) * 64, 64), pl.ds((i // 2) * 64, 64)]
            copies.append(pltpu.make_async_copy(piece, to, in_sems.at[4 * j + i]))
    for copy in copies:
        copy.start()

    stops = []
    stop = 0
    for which, most in enumerate(BUCKETS):
        below = BUCKETS[which + 1] if which + 1 < len(BUCKETS) else 0

        def place(g, at, most=most, below=below):
            count = count_ref[4 * g + mine]
            inside = jnp.logical_and(count <= most, count > below)

            @pl.when(inside)
            def _():
                order_ref[at] = g

            return at + inside.astype(jnp.int32)

        stop = lax.fori_loop(0, GROUPS, place, jnp.int32(stop))
        stops.append(stop)

    @pl.loop(0, 128)
    def _(t):
        acc[t] = jnp.zeros((128, 256), jnp.float32)

    gain_query = gains_ref[0:1, :]
    gain_ref[...] = jnp.zeros_like(gain_ref)
    for copy in copies:
        copy.wait()

    zero = jnp.zeros((128, 128), jnp.bfloat16)

    def forward(i, most, first):
        g = order_ref[i]
        live = count_ref[4 * g + mine]
        listed = [list_ref[(4 * g + mine) * 8 + j] for j in range(most)]
        spots = [((c & 1) ^ chip) * 64 + (c >> 1) for c in listed]
        wide = jnp.concatenate([qg_ref[2 * g, 0], qg_ref[2 * g + 1, 0]], axis=0).astype(jnp.float32)
        grad = jnp.concatenate([qg_ref[2 * g, 1], qg_ref[2 * g + 1, 1]], axis=0)
        scale = lax.rsqrt(jnp.mean(wide * wide, axis=-1, keepdims=True) + EPS)
        hat = wide * scale
        normed = (hat * gain_query).astype(jnp.bfloat16)
        keys = jnp.concatenate([ktab[t] for t in spots], axis=0)
        values = jnp.concatenate([vtab[t] for t in spots], axis=0)
        flat = dot(normed, keys, NT)
        scores = []
        for j in range(most):
            s = flat[:, j * 128:(j + 1) * 128]
            if j == most - 1 or (j and not first):
                s = jnp.where(j < live, s, -jnp.inf)
            scores.append(s)
        top = jnp.max(functools.reduce(jnp.maximum, scores), axis=-1, keepdims=True)
        exps = [jnp.exp2((s - top) * (INV_ROOT * LOG2E)) for s in scores]
        total = jnp.sum(functools.reduce(jnp.add, exps), axis=-1, keepdims=True)
        inverse = 1.0 / total
        weights = [(e * inverse).astype(jnp.bfloat16) for e in exps]
        attended = dot(jnp.concatenate(weights, axis=1), values, NN).astype(jnp.bfloat16)
        og_ref[2 * g, 0] = attended[:64]
        og_ref[2 * g + 1, 0] = attended[64:]
        inner = jnp.sum(grad.astype(jnp.float32) * attended.astype(jnp.float32), axis=-1, keepdims=True)
        return g, spots, wide, grad, scale, hat, normed, keys, values, weights, inner

    def backward(state, most):
        g, spots, wide, grad, scale, hat, normed, keys, values, weights, inner = state
        flat = dot(grad, values, NT)
        score_grads = []
        for j in range(most):
            wg = flat[:, j * 128:(j + 1) * 128]
            score_grads.append((weights[j].astype(jnp.float32) * (wg - inner)).astype(jnp.bfloat16))
        norm_grad = dot(jnp.concatenate(score_grads, axis=1), keys, NN) * INV_ROOT
        pair = jnp.concatenate(
            [jnp.concatenate([normed, zero], axis=1), jnp.concatenate([zero, grad], axis=1)], axis=0
        )
        for j in range(most):
            acc[spots[j]] += dot(jnp.concatenate([score_grads[j], weights[j]], axis=0), pair, TN)
        gain_ref[0:1, :] += jnp.sum(norm_grad * hat, axis=0, keepdims=True)
        weighted = norm_grad * gain_query
        mean = jnp.mean(weighted * wide, axis=-1, keepdims=True)
        query_grad = (scale * weighted - wide * (scale * scale * scale) * mean).astype(jnp.bfloat16)
        og_ref[2 * g, 1] = query_grad[:64]
        og_ref[2 * g + 1, 1] = query_grad[64:]

    start = 0
    for which, most in enumerate(BUCKETS):
        stop = (stops[which] + TOGETHER - 1) // TOGETHER

        @pl.loop(start, stop)
        def _(step, most=most):
            states = [forward(step * TOGETHER + u, most, u == 0) for u in range(TOGETHER)]
            for state in states:
                backward(state, most)

        start = stop

    back = [pltpu.make_async_copy(og_ref, og_hbm, out_sems.at[16])]
    back[0].start()
    outs = (p0, p1, p2, p3)
    for part in range(4):

        @pl.loop(part * 16, part * 16 + 16)
        def _(s):
            for x in range(2):
                both = acc[x * 64 + s]
                k = (both[:, :128] * INV_ROOT).astype(jnp.bfloat16)
                v = both[:, 128:].astype(jnp.bfloat16)
                for c in range(2):
                    stage[2 * c + x, s, 0] = k[c * 64:(c + 1) * 64]
                    stage[2 * c + x, s, 1] = v[c * 64:(c + 1) * 64]

        for i, out in enumerate(outs):
            rows = pl.ds(part * 16, 16)
            back.append(pltpu.make_async_copy(stage.at[i, rows], out.at[rows], out_sems.at[part * 4 + i]))
            back[-1].start()
    for copy in back:
        copy.wait()


def attend(info, counts, lists, keys, values, qg, gains):
    smem = pl.BlockSpec(memory_space=pltpu.SMEM)
    vmem = pl.BlockSpec(memory_space=pltpu.VMEM)
    hbm = pl.BlockSpec(memory_space=pl.ANY)
    piece = jax.ShapeDtypeStruct((64, 2, 64, 128), jnp.bfloat16)
    return pl.pallas_call(
        attend_kernel,
        out_shape=(piece, piece, piece, piece, piece, jax.ShapeDtypeStruct((8, 128), jnp.float32)),
        in_specs=[smem] * 3 + [hbm] * 9 + [vmem],
        out_specs=(hbm,) * 5 + (vmem,),
        scratch_shapes=[
            pltpu.VMEM((128, 128, 128), jnp.bfloat16),
            pltpu.VMEM((128, 128, 128), jnp.bfloat16),
            pltpu.VMEM((128, 128, 256), jnp.float32),
            pltpu.VMEM((64, 2, 64, 128), jnp.bfloat16),
            pltpu.VMEM((64, 2, 64, 128), jnp.bfloat16),
            pltpu.VMEM((4, 64, 2, 64, 128), jnp.bfloat16),
            pltpu.SMEM((GROUPS,), jnp.int32),
            pltpu.SemaphoreType.DMA((9,)),
            pltpu.SemaphoreType.DMA((17,)),
        ],
        compiler_params=pltpu.CompilerParams(vmem_limit_bytes=56 * 1024 * 1024),
        cost_estimate=pl.CostEstimate(flops=6 * 10**9, bytes_accessed=20 * 2**20, transcendentals=4 * 2**20),
        name="attend",
    )(info, counts, lists, *keys, *values, qg, gains)


HEADS = 16


def finish_kernel(own_ref, core_ref, far_ref, kv_ref, gain_ref, out_ref, row_ref):
    @pl.when(pl.program_id(0) == 0)
    def _():
        row_ref[...] = jnp.zeros_like(row_ref)

    gain = gain_ref[0:1, :]

    @pl.loop(0, own_ref.shape[0], unroll=2)
    def _(s):
        total = own_ref[s].astype(jnp.float32) + core_ref[s].astype(jnp.float32) + far_ref[s].astype(jnp.float32)
        out_ref[s, 1] = total[1].astype(jnp.bfloat16)
        total = total[0]
        wide = kv_ref[s, 0].astype(jnp.float32)
        scale = lax.rsqrt(jnp.mean(wide * wide, axis=-1, keepdims=True) + EPS)
        weighted = total * gain
        inner = jnp.mean(weighted * wide, axis=-1, keepdims=True)
        out_ref[s, 0] = (scale * weighted - wide * (scale * scale * scale) * inner).astype(jnp.bfloat16)
        row_ref[0:1, :] += jnp.sum(total * (wide * scale), axis=0, keepdims=True)


def finish(own, core, far, kv, gain):
    block = pl.BlockSpec((8, 2, 64, 128), lambda i: (i, 0, 0, 0))
    first = pl.BlockSpec((8, 1, 64, 128), lambda i: (i, 0, 0, 0))
    whole = pl.BlockSpec((1, 128), lambda i: (0, 0))
    return pl.pallas_call(
        finish_kernel,
        grid=(8,),
        out_shape=(jax.ShapeDtypeStruct((64, 2, 64, 128), jnp.bfloat16), jax.ShapeDtypeStruct((8, 128), jnp.float32)),
        in_specs=[block, block, block, first, whole],
        out_specs=(block, pl.BlockSpec((8, 128), lambda i: (0, 0))),
        name="finish",
    )(own, core, far, kv, gain)


def unpack_kernel(in_ref, a_ref, b_ref):
    for i, out in enumerate((a_ref, b_ref)):
        for h in range(4):
            for r in range(4):
                out[r * 64:(r + 1) * 64, h * 128:(h + 1) * 128] = in_ref[h * 4 + r, i]


def unpack(pieces):
    rows = jax.ShapeDtypeStruct((256, HEADS * HEAD_DIM), jnp.bfloat16)
    return pl.pallas_call(
        unpack_kernel,
        grid=(4,),
        out_shape=(rows, rows),
        in_specs=[pl.BlockSpec((16, 2, 64, 128), lambda i: (i, 0, 0, 0))],
        out_specs=(pl.BlockSpec((256, 512), lambda i: (0, i)),) * 2,
        cost_estimate=pl.CostEstimate(flops=0, bytes_accessed=2**22, transcendentals=0),
        name="unpack",
    )(pieces)


def unpack_front_kernel(core_ref, in_ref, got_ref, a_ref, b_ref):
    core = core_ref[0]
    for i, out in enumerate((a_ref, b_ref)):
        for h in range(4):
            for block in range(2):
                near = pl.multiple_of(block * 128 + core * 64, 64)
                away = pl.multiple_of(block * 128 + (1 - core) * 64, 64)
                out[pl.ds(near, 64), h * 128:(h + 1) * 128] = in_ref[h * 4 + 2 * core + block, i]
                out[pl.ds(away, 64), h * 128:(h + 1) * 128] = got_ref[h, block, i]


def unpack_front(core, pieces, got):
    rows = jax.ShapeDtypeStruct((256, HEADS * HEAD_DIM), jnp.bfloat16)
    return pl.pallas_call(
        unpack_front_kernel,
        grid=(4,),
        out_shape=(rows, rows),
        in_specs=[
            pl.BlockSpec(memory_space=pltpu.SMEM),
            pl.BlockSpec((16, 2, 64, 128), lambda i: (i, 0, 0, 0)),
            pl.BlockSpec((4, 2, 2, 64, 128), lambda i: (i, 0, 0, 0, 0)),
        ],
        out_specs=(pl.BlockSpec((256, 512), lambda i: (0, i)),) * 2,
        cost_estimate=pl.CostEstimate(flops=0, bytes_accessed=2**22, transcendentals=0),
        name="unpack_front",
    )(core.reshape(1), pieces, got)


def to_send(rows):
    return jnp.transpose(rows.reshape(4, 64, HEADS, HEAD_DIM), (2, 0, 1, 3)).reshape(64, 64, HEAD_DIM)


def exchange(array):
    return lax.all_to_all(array, "seq", split_axis=0, concat_axis=0, tiled=True)


def across(array, flip):
    return lax.ppermute(array, "seq", [(i, i ^ flip) for i in range(64)])


def halves_swapped(rows, core):
    shaped = rows.reshape(2, 2, 64, HEADS * HEAD_DIM)
    kept = jnp.where(core == 0, shaped[:, 0], shaped[:, 1])
    given = jnp.where(core == 0, shaped[:, 1], shaped[:, 0])
    got = across(given, 1)
    return jnp.concatenate([jnp.where(core == 0, kept, got), jnp.where(core == 0, got, kept)])


def over_copies(row):
    for flip in (1, 2):
        row = row + lax.ppermute(row, "dp", [(i, i ^ flip) for i in range(4)])
    for flip in (1, 2):
        row = row + across(row, flip)
    return row


def body(query_rows, key_rows, value_rows, output_grad, query_gain, key_gain, block_list, block_count):
    position = lax.axis_index("seq")
    head = position // 4
    chip = position // 2 % 2
    core = position % 2
    lists = lax.dynamic_slice_in_dim(block_list[0], head, 1, 0).reshape(1024)
    counts = lax.dynamic_slice_in_dim(block_count[0], head, 1, 0).reshape(128)
    info = jnp.stack([position % 4, chip]).astype(jnp.int32)
    gain_query = lax.dynamic_slice_in_dim(query_gain, head, 1, 0)
    gain_key = lax.dynamic_slice_in_dim(key_gain, head, 1, 0)

    with jax.named_scope("gather"):
        kv_own = exchange(jnp.stack([to_send(key_rows[0]), to_send(value_rows[0])], axis=1))
        pair_send = jnp.stack(
            [to_send(halves_swapped(query_rows[0], core)), to_send(halves_swapped(output_grad[0], core))], axis=1
        )
        pair_send, kv_own, lists, counts, info = lax.optimization_barrier((pair_send, kv_own, lists, counts, info))
        value_own = kv_own[:, 1]
        value_chip = across(value_own, 2)
        wide = kv_own[:, 0].astype(jnp.float32)
        scale = lax.rsqrt(jnp.mean(wide * wide, axis=-1, keepdims=True) + EPS)
        key_own = (wide * scale * gain_key).astype(jnp.bfloat16)
        key_chip = across(key_own, 2)
        query_pair = exchange(pair_send)
        keys = (key_own, key_chip, across(key_own, 1), across(key_chip, 1))
        values = (value_own, value_chip, across(value_own, 1), across(value_chip, 1))
    with jax.named_scope("attend"):
        outs = attend(info, counts, lists, keys, values, query_pair, gain_query)
    front, part_own, part_chip, part_core, part_far, query_row = outs
    with jax.named_scope("return"):
        far = (part_chip.astype(jnp.float32) + across(part_far, 1).astype(jnp.float32)).astype(jnp.bfloat16)
        near = across(part_core, 1)
        front, far = lax.optimization_barrier((front, far))
        far = across(far, 2)
        front = exchange(front)
        given = front.reshape(HEADS, 2, 2, 2, 64, HEAD_DIM)
        got = across(jnp.where(core == 0, given[:, 1], given[:, 0]), 1)
        attended, query_grad = unpack_front(core, front, got)
        kv_grad, key_row = finish(part_own, near, far, kv_own, gain_key)
        key_grad, value_grad = unpack(exchange(kv_grad))
    with jax.named_scope("gains"):
        rows = jnp.concatenate([over_copies(query_row[0:1]), over_copies(key_row[0:1])])
        other = across(rows, 4)
        low = position // 4 % 2 == 0
        rows = jnp.where(low, jnp.stack([rows, other]), jnp.stack([other, rows]))
        turns = [rows] + [lax.ppermute(rows, "seq", [(i, (i + 8 * d) % 64) for i in range(64)]) for d in range(1, 8)]
        turns = jnp.stack(turns[::-1] + turns[::-1])
        turns = lax.dynamic_slice_in_dim(turns, 7 - position // 8, 8, 0).reshape(HEADS, 2, HEAD_DIM)
    return (attended[None], query_grad[None], key_grad[None], value_grad[None], turns[:, 0], turns[:, 1])


def solution(mesh):
    rows = P("dp", "seq", None)
    return jax.shard_map(
        body,
        mesh=mesh,
        in_specs=(rows, rows, rows, rows, P(), P(), P("dp", None, None, None), P("dp", None, None)),
        out_specs=(rows, rows, rows, rows, P(), P()),
        check_vma=False,
    )
```

```python
import functools
import math

import jax
import jax.numpy as jnp
from jax import lax
from jax.experimental import pallas as pl
from jax.experimental.pallas import tpu as pltpu
from jax.sharding import PartitionSpec as P

HEAD_DIM = 128
EPS = 1e-06
INV_ROOT = 1.0 / math.sqrt(HEAD_DIM)
LOG2E = math.log2(math.e)
NT = (((1,), (1,)), ((), ()))
TN = (((0,), (0,)), ((), ()))
NN = (((1,), (0,)), ((), ()))
GROUPS = 32
BUCKETS = (8, 6, 4, 2)
TOGETHER = 1
SEND_ORDER = (5, 3, 1, 7, 4, 2, 0, 6)


def dot(a, b, dims):
    return lax.dot_general(a, b, dims, preferred_element_type=jnp.float32)


def attend_kernel(info_ref, count_ref, list_ref, *refs):
    pieces = refs[:8]
    qg_hbm, gains_ref, og_hbm = refs[8:11]
    parts = refs[11:19]
    gain_query_ref, gain_key_ref, ktab, vtab, acc, qg_ref, og_ref, stage, order_ref, in_sems, out_sems = refs[19:]
    place_x_core = info_ref[0]
    head = info_ref[1]
    copies = [pltpu.make_async_copy(qg_hbm, qg_ref, in_sems.at[16])]
    for i, piece in enumerate(pieces):
        for j, table in enumerate((ktab, vtab)):
            copies.append(pltpu.make_async_copy(piece.at[j], table.at[pl.ds(i * 16, 16)], in_sems.at[2 * i + j]))
    for copy in copies:
        copy.start()

    def block_of(g):
        across = place_x_core ^ (6 * ((g >> 1) & 1))
        return (g >> 2) * 16 + across * 2 + (g & 1)

    stops = []
    stop = 0
    for which, most in enumerate(BUCKETS):
        below = BUCKETS[which + 1] if which + 1 < len(BUCKETS) else 0

        def place(g, at, most=most, below=below):
            count = count_ref[block_of(g)]
            inside = jnp.logical_and(count <= most, count > below)

            @pl.when(inside)
            def _():
                order_ref[at] = g

            return at + inside.astype(jnp.int32)

        stop = lax.fori_loop(0, GROUPS, place, jnp.int32(stop))
        stops.append(stop)

    @pl.loop(0, 128)
    def _(t):
        acc[t] = jnp.zeros((128, 256), jnp.float32)

    gain_query = gains_ref[pl.ds(head, 1), :]
    gain_key = gains_ref[pl.ds(16 + head, 1), :]
    gain_query_ref[...] = jnp.zeros_like(gain_query_ref)
    gain_key_ref[...] = jnp.zeros_like(gain_key_ref)
    for copy in copies:
        copy.wait()

    zero = jnp.zeros((128, 128), jnp.bfloat16)

    def forward(i, most, first):
        g = order_ref[i]
        block = block_of(g)
        live = count_ref[block]
        listed = [list_ref[block * 8 + j] for j in range(most)]
        spots = [(((c >> 1) & 7) ^ place_x_core) * 16 + (c >> 4) * 2 + (c & 1) for c in listed]
        wide = qg_ref[g >> 1, 0, g & 1].astype(jnp.float32)
        grad = qg_ref[g >> 1, 1, g & 1]
        scale = lax.rsqrt(jnp.mean(wide * wide, axis=-1, keepdims=True) + EPS)
        hat = wide * scale
        normed = (hat * gain_query).astype(jnp.bfloat16)
        keys = jnp.concatenate([ktab[t] for t in spots], axis=0)
        values = jnp.concatenate([vtab[t] for t in spots], axis=0)
        flat = dot(normed, keys, NT)
        scores = []
        for j in range(most):
            s = flat[:, j * 128:(j + 1) * 128]
            if j == most - 1 or (j and not first):
                s = jnp.where(j < live, s, -jnp.inf)
            scores.append(s)
        top = jnp.max(functools.reduce(jnp.maximum, scores), axis=-1, keepdims=True)
        exps = [jnp.exp2((s - top) * (INV_ROOT * LOG2E)) for s in scores]
        total = jnp.sum(functools.reduce(jnp.add, exps), axis=-1, keepdims=True)
        inverse = 1.0 / total
        weights = [(e * inverse).astype(jnp.bfloat16) for e in exps]
        attended = dot(jnp.concatenate(weights, axis=1), values, NN).astype(jnp.bfloat16)
        og_ref[g >> 1, 0, g & 1] = attended
        inner = jnp.sum(grad.astype(jnp.float32) * attended.astype(jnp.float32), axis=-1, keepdims=True)
        return g, spots, wide, grad, scale, hat, normed, keys, values, weights, inner

    def backward(state, most):
        g, spots, wide, grad, scale, hat, normed, keys, values, weights, inner = state
        flat = dot(grad, values, NT)
        score_grads = []
        for j in range(most):
            wg = flat[:, j * 128:(j + 1) * 128]
            score_grads.append((weights[j].astype(jnp.float32) * (wg - inner)).astype(jnp.bfloat16))
        norm_grad = dot(jnp.concatenate(score_grads, axis=1), keys, NN) * INV_ROOT
        pair = jnp.concatenate(
            [jnp.concatenate([normed, zero], axis=1), jnp.concatenate([zero, grad], axis=1)], axis=0
        )
        for j in range(most):
            acc[spots[j]] += dot(jnp.concatenate([score_grads[j], weights[j]], axis=0), pair, TN)
        gain_query_ref[0:1, :] += jnp.sum(norm_grad * hat, axis=0, keepdims=True)
        weighted = norm_grad * gain_query
        mean = jnp.mean(weighted * wide, axis=-1, keepdims=True)
        og_ref[g >> 1, 1, g & 1] = (scale * weighted - wide * (scale * scale * scale) * mean).astype(jnp.bfloat16)

    start = 0
    for which, most in enumerate(BUCKETS):
        stop = (stops[which] + TOGETHER - 1) // TOGETHER

        @pl.loop(start, stop)
        def _(step, most=most):
            states = [forward(step * TOGETHER + u, most, u == 0) for u in range(TOGETHER)]
            for state in states:
                backward(state, most)

        start = stop

    back = [pltpu.make_async_copy(og_ref, og_hbm, out_sems.at[8])]
    back[0].start()
    for i in SEND_ORDER:

        @pl.loop(i * 16, i * 16 + 16, unroll=2)
        def _(t, i=i):
            both = acc[t]
            k = (both[:, :128] * INV_ROOT).astype(jnp.bfloat16)
            stage[i, 0, t - i * 16] = k
            stage[i, 1, t - i * 16] = both[:, 128:].astype(jnp.bfloat16)
            sums = jnp.sum(k.astype(jnp.float32) * ktab[t].astype(jnp.float32), axis=0, keepdims=True)
            gain_key_ref[0:1, :] += sums

        back.append(pltpu.make_async_copy(stage.at[i], parts[i], out_sems.at[i]))
        back[-1].start()
    gain_key_ref[0:1, :] = gain_key_ref[0:1, :] / gain_key
    for copy in back:
        copy.wait()


def attend(info, counts, lists, pieces, qg, gains):
    smem = pl.BlockSpec(memory_space=pltpu.SMEM)
    vmem = pl.BlockSpec(memory_space=pltpu.VMEM)
    hbm = pl.BlockSpec(memory_space=pl.ANY)
    part = jax.ShapeDtypeStruct((2, 16, 128, 128), jnp.bfloat16)
    row = jax.ShapeDtypeStruct((8, 128), jnp.float32)
    return pl.pallas_call(
        attend_kernel,
        out_shape=(jax.ShapeDtypeStruct((16, 2, 2, 128, 128), jnp.bfloat16),) + (part,) * 8 + (row, row),
        in_specs=[smem] * 3 + [hbm] * 9 + [vmem],
        out_specs=(hbm,) * 9 + (vmem,) * 2,
        scratch_shapes=[
            pltpu.VMEM((128, 128, 128), jnp.bfloat16),
            pltpu.VMEM((128, 128, 128), jnp.bfloat16),
            pltpu.VMEM((128, 128, 256), jnp.float32),
            pltpu.VMEM((16, 2, 2, 128, 128), jnp.bfloat16),
            pltpu.VMEM((16, 2, 2, 128, 128), jnp.bfloat16),
            pltpu.VMEM((8, 2, 16, 128, 128), jnp.bfloat16),
            pltpu.SMEM((GROUPS,), jnp.int32),
            pltpu.SemaphoreType.DMA((17,)),
            pltpu.SemaphoreType.DMA((9,)),
        ],
        compiler_params=pltpu.CompilerParams(vmem_limit_bytes=56 * 1024 * 1024),
        cost_estimate=pl.CostEstimate(flops=6 * 10**9, bytes_accessed=20 * 2**20, transcendentals=4 * 2**20),
        name="attend",
    )(info, counts, lists, *pieces, qg, gains)


HEADS = 16
ALONG_Z = [[8 * z + rest for z in range(8)] for rest in range(8)]


def finish_kernel(mine_ref, part_ref, core_ref, side_ref, far_ref, kv_ref, gain_ref, out_ref):
    half = mine_ref[0]
    plane = mine_ref[1]
    for own in (True, False):
        hh = half if own else 1 - half
        gain = gain_ref[pl.ds(2 * plane + hh, 1), :]
        if own:
            total = [part_ref[i, 0].astype(jnp.float32) + core_ref[i, 0].astype(jnp.float32) + side_ref[i, 0].astype(jnp.float32)
                     for i in range(2)]
        else:
            total = [far_ref[i, 0].astype(jnp.float32) for i in range(2)]
        wide = kv_ref[0, hh, 0].astype(jnp.float32)
        scale = lax.rsqrt(jnp.mean(wide * wide, axis=-1, keepdims=True) + EPS)
        weighted = total[0] * gain
        inner = jnp.mean(weighted * wide, axis=-1, keepdims=True)
        out_ref[0, hh, 0] = (scale * weighted - wide * (scale * scale * scale) * inner).astype(jnp.bfloat16)
        out_ref[0, hh, 1] = total[1].astype(jnp.bfloat16)


def finish(mine, part, core, side, far, kv, gain):
    piece = pl.BlockSpec((2, 1, 256, 128), lambda i: (0, i, 0, 0))
    return pl.pallas_call(
        finish_kernel,
        grid=(8,),
        out_shape=jax.ShapeDtypeStruct((8, 2, 2, 256, 128), jnp.bfloat16),
        in_specs=[pl.BlockSpec(memory_space=pltpu.SMEM), piece, piece, piece, piece,
                  pl.BlockSpec((1, 2, 1, 256, 128), lambda i: (i, 0, 0, 0, 0)),
                  pl.BlockSpec((HEADS, 128), lambda i: (0, 0))],
        out_specs=pl.BlockSpec((1, 2, 2, 256, 128), lambda i: (i, 0, 0, 0, 0)),
        name="finish",
    )(mine, part, core, side, far, kv, gain)


def unpack_kernel(in_ref, a_ref, b_ref):
    for i, out in enumerate((a_ref, b_ref)):
        for z in range(2):
            for hh in range(2):
                h = 2 * z + hh
                out[:, h * 128:(h + 1) * 128] = in_ref[z, hh, i]


def unpack(pieces):
    rows = jax.ShapeDtypeStruct((256, HEADS * HEAD_DIM), jnp.bfloat16)
    return pl.pallas_call(
        unpack_kernel,
        grid=(4,),
        out_shape=(rows, rows),
        in_specs=[pl.BlockSpec((2, 2, 2, 256, 128), lambda i: (i, 0, 0, 0, 0))],
        out_specs=(pl.BlockSpec((256, 512), lambda i: (0, i)),) * 2,
        cost_estimate=pl.CostEstimate(flops=0, bytes_accessed=2**22, transcendentals=0),
        name="unpack",
    )(pieces)


def unpack_front_kernel(mine_ref, in_ref, got_ref, a_ref, b_ref):
    half = mine_ref[0]
    for i, out in enumerate((a_ref, b_ref)):
        for z in range(2):
            here = pl.multiple_of((2 * z + half) * 128, 128)
            there = pl.multiple_of((2 * z + 1 - half) * 128, 128)
            out[:, pl.ds(here, 128)] = in_ref[z, 0, i]
            out[:, pl.ds(there, 128)] = got_ref[z, i]


def unpack_front(mine, pieces, got):
    rows = jax.ShapeDtypeStruct((256, HEADS * HEAD_DIM), jnp.bfloat16)
    return pl.pallas_call(
        unpack_front_kernel,
        grid=(4,),
        out_shape=(rows, rows),
        in_specs=[
            pl.BlockSpec(memory_space=pltpu.SMEM),
            pl.BlockSpec((2, 1, 2, 256, 128), lambda i: (i, 0, 0, 0, 0)),
            pl.BlockSpec((2, 2, 256, 128), lambda i: (i, 0, 0, 0)),
        ],
        out_specs=(pl.BlockSpec((256, 512), lambda i: (0, i)),) * 2,
        cost_estimate=pl.CostEstimate(flops=0, bytes_accessed=2**22, transcendentals=0),
        name="unpack_front",
    )(mine, pieces, got)


def along_z(array):
    return lax.all_to_all(array, "seq", split_axis=0, concat_axis=0, axis_index_groups=ALONG_Z, tiled=True)


def across(array, flip):
    return lax.ppermute(array, "seq", [(i, i ^ flip) for i in range(64)])


def by_head(rows):
    return jnp.transpose(rows.reshape(256, 8, 2, HEAD_DIM), (1, 2, 0, 3))


def wide_sum(*arrays):
    return functools.reduce(jnp.add, [a.astype(jnp.float32) for a in arrays]).astype(jnp.bfloat16)


def over_copies(row):
    for flip in (1, 2):
        row = row + lax.ppermute(row, "dp", [(i, i ^ flip) for i in range(4)])
    for flip in (1, 2):
        row = row + across(row, flip)
    return row


def body(query_rows, key_rows, value_rows, output_grad, query_gain, key_gain, block_list, block_count):
    position = lax.axis_index("seq")
    head = position // 4
    plane = position // 8
    half = head % 2
    lists = lax.dynamic_slice_in_dim(block_list[0], head, 1, 0).reshape(1024)
    counts = lax.dynamic_slice_in_dim(block_count[0], head, 1, 0).reshape(128)
    info = jnp.stack([position % 8, head]).astype(jnp.int32)
    mine = jnp.stack([half, plane]).astype(jnp.int32)
    gains = jnp.concatenate([query_gain, key_gain])

    def of_half(pair, which):
        return jnp.where(which == 0, pair[:, 0], pair[:, 1])

    with jax.named_scope("gather"):
        query_heads, grad_heads = by_head(query_rows[0]), by_head(output_grad[0])
        given = jnp.stack([of_half(query_heads, 1 - half), of_half(grad_heads, 1 - half)], axis=1)
        got = across(given, 6)
        kept = jnp.stack([of_half(query_heads, half), of_half(grad_heads, half)], axis=1)
        kv = along_z(jnp.stack([by_head(key_rows[0]), by_head(value_rows[0])], axis=2))
        pair_send = jnp.stack([kept, got], axis=1)
        pair_send, kv, lists, counts, info, mine, gains = lax.optimization_barrier(
            (pair_send, kv, lists, counts, info, mine, gains)
        )
        wide = kv[:, :, 0].astype(jnp.float32)
        scale = lax.rsqrt(jnp.mean(wide * wide, axis=-1, keepdims=True) + EPS)
        pair_gain = lax.dynamic_slice_in_dim(key_gain, 2 * plane, 2, 0)
        normed = (wide * scale * pair_gain[None, :, None, :]).astype(jnp.bfloat16)
        values = kv[:, :, 1]
        cross_send = jnp.stack([of_half(normed, 1 - half), of_half(values, 1 - half)])
        own = jnp.stack([of_half(normed, half), of_half(values, half)])
        cross = across(cross_send, 6)
        side = across(own, 2)
        query_pair = along_z(pair_send)
        far = across(cross, 2)
        pieces = []
        for piece in (own, side, far, cross):
            pieces += [piece, across(piece, 1)]
        pieces = [p.reshape(2, 16, 128, 128) for p in pieces]
    with jax.named_scope("attend"):
        outs = attend(info, counts, lists, pieces, query_pair.reshape(16, 2, 2, 128, 128), gains)
    front, parts, query_row, key_row = outs[0], outs[1:9], outs[9], outs[10]
    with jax.named_scope("return"):
        far = wide_sum(parts[4], across(parts[5], 1))
        side = wide_sum(parts[2], across(parts[3], 1))
        front, far, side = lax.optimization_barrier((front, far, side))
        front = along_z(front.reshape(8, 2, 2, 256, HEAD_DIM))
        far = across(far, 2)
        side = across(side, 2)
        cross = across(wide_sum(parts[6], across(parts[7], 1), far), 6)
        core = across(parts[1], 1)
        shape = (2, 8, 256, HEAD_DIM)
        kv_grad = finish(mine, parts[0].reshape(shape), core.reshape(shape), side.reshape(shape), cross.reshape(shape), kv, key_gain)
        got = across(front[:, 1], 6)
        attended, query_grad = unpack_front(mine, front, got)
        key_grad, value_grad = unpack(along_z(kv_grad))
    with jax.named_scope("gains"):
        rows = over_copies(jnp.concatenate([query_row[0:1], key_row[0:1]]))
        other = across(rows, 4)
        rows = jnp.where(half == 0, jnp.stack([rows, other]), jnp.stack([other, rows]))
        turns = [rows] + [lax.ppermute(rows, "seq", [(i, (i + 8 * d) % 64) for i in range(64)]) for d in range(1, 8)]
        turns = jnp.stack(turns[::-1] + turns[::-1])
        turns = lax.dynamic_slice_in_dim(turns, 7 - plane, 8, 0).reshape(HEADS, 2, HEAD_DIM)
    return (attended[None], query_grad[None], key_grad[None], value_grad[None], turns[:, 0], turns[:, 1])


def solution(mesh):
    rows = P("dp", "seq", None)
    return jax.shard_map(
        body,
        mesh=mesh,
        in_specs=(rows, rows, rows, rows, P(), P(), P("dp", None, None, None), P("dp", None, None)),
        out_specs=(rows, rows, rows, rows, P(), P()),
        check_vma=False,
    )
```

```python
import functools
import math

import jax
import jax.numpy as jnp
from jax import lax
from jax.experimental import pallas as pl
from jax.experimental.pallas import tpu as pltpu
from jax.sharding import PartitionSpec as P

HEAD_DIM = 128
EPS = 1e-06
INV_ROOT = 1.0 / math.sqrt(HEAD_DIM)
LOG2E = math.log2(math.e)
NT = (((1,), (1,)), ((), ()))
TN = (((0,), (0,)), ((), ()))
NN = (((1,), (0,)), ((), ()))
GROUPS = 32
BUCKETS = (8, 6, 4, 2)
TOGETHER = 1
SEND_ORDER = (5, 3, 1, 7, 4, 2, 0, 6)


def dot(a, b, dims):
    return lax.dot_general(a, b, dims, preferred_element_type=jnp.float32)


def attend_kernel(info_ref, count_ref, list_ref, *refs):
    pieces = refs[:8]
    qg_hbm, query_gain_ref, key_gain_ref, og_hbm = refs[8:12]
    parts = refs[12:20]
    gain_query_ref, gain_key_ref, ktab, vtab, acc, qg_ref, og_ref, stage, order_ref, in_sems, out_sems = refs[20:]
    place_x_core = info_ref[0]
    head = info_ref[1]
    copies = [pltpu.make_async_copy(qg_hbm, qg_ref, in_sems.at[16])]
    for i, piece in enumerate(pieces):
        for j, table in enumerate((ktab, vtab)):
            copies.append(pltpu.make_async_copy(piece.at[j], table.at[pl.ds(i * 16, 16)], in_sems.at[2 * i + j]))
    for copy in copies:
        copy.start()

    def block_of(g):
        across = place_x_core ^ (6 * ((g >> 1) & 1))
        return (g >> 2) * 16 + across * 2 + (g & 1)

    stops = []
    stop = 0
    for which, most in enumerate(BUCKETS):
        below = BUCKETS[which + 1] if which + 1 < len(BUCKETS) else 0

        def place(g, at, most=most, below=below):
            count = count_ref[block_of(g)]
            inside = jnp.logical_and(count <= most, count > below)

            @pl.when(inside)
            def _():
                order_ref[at] = g

            return at + inside.astype(jnp.int32)

        stop = lax.fori_loop(0, GROUPS, place, jnp.int32(stop))
        stops.append(stop)

    @pl.loop(0, 128)
    def _(t):
        acc[t] = jnp.zeros((128, 256), jnp.float32)

    gain_query = query_gain_ref[pl.ds(head, 1), :]
    gain_key = key_gain_ref[pl.ds(head, 1), :]
    gain_query_ref[...] = jnp.zeros_like(gain_query_ref)
    gain_key_ref[...] = jnp.zeros_like(gain_key_ref)
    for copy in copies:
        copy.wait()

    zero = jnp.zeros((128, 128), jnp.bfloat16)

    def forward(i, most, first):
        g = order_ref[i]
        block = block_of(g)
        live = count_ref[block]
        listed = [list_ref[block * 8 + j] for j in range(most)]
        spots = [(((c >> 1) & 7) ^ place_x_core) * 16 + (c >> 4) * 2 + (c & 1) for c in listed]
        wide = qg_ref[g >> 1, 0, g & 1].astype(jnp.float32)
        grad = qg_ref[g >> 1, 1, g & 1]
        scale = lax.rsqrt(jnp.mean(wide * wide, axis=-1, keepdims=True) + EPS)
        hat = wide * scale
        normed = (hat * gain_query).astype(jnp.bfloat16)
        keys = jnp.concatenate([ktab[t] for t in spots], axis=0)
        values = jnp.concatenate([vtab[t] for t in spots], axis=0)
        flat = dot(normed, keys, NT)
        scores = []
        for j in range(most):
            s = flat[:, j * 128:(j + 1) * 128]
            if j == most - 1 or (j and not first):
                s = jnp.where(j < live, s, -jnp.inf)
            scores.append(s)
        top = jnp.max(functools.reduce(jnp.maximum, scores), axis=-1, keepdims=True)
        exps = [jnp.exp2((s - top) * (INV_ROOT * LOG2E)) for s in scores]
        total = jnp.sum(functools.reduce(jnp.add, exps), axis=-1, keepdims=True)
        inverse = 1.0 / total
        weights = [(e * inverse).astype(jnp.bfloat16) for e in exps]
        attended = dot(jnp.concatenate(weights, axis=1), values, NN).astype(jnp.bfloat16)
        og_ref[g >> 1, 0, g & 1] = attended
        inner = jnp.sum(grad.astype(jnp.float32) * attended.astype(jnp.float32), axis=-1, keepdims=True)
        return g, spots, wide, grad, scale, hat, normed, keys, values, weights, inner

    def backward(state, most):
        g, spots, wide, grad, scale, hat, normed, keys, values, weights, inner = state
        flat = dot(grad, values, NT)
        score_grads = []
        for j in range(most):
            wg = flat[:, j * 128:(j + 1) * 128]
            score_grads.append((weights[j].astype(jnp.float32) * (wg - inner)).astype(jnp.bfloat16))
        norm_grad = dot(jnp.concatenate(score_grads, axis=1), keys, NN) * INV_ROOT
        pair = jnp.concatenate(
            [jnp.concatenate([normed, zero], axis=1), jnp.concatenate([zero, grad], axis=1)], axis=0
        )
        for j in range(most):
            acc[spots[j]] += dot(jnp.concatenate([score_grads[j], weights[j]], axis=0), pair, TN)
        gain_query_ref[0:1, :] += jnp.sum(norm_grad * hat, axis=0, keepdims=True)
        weighted = norm_grad * gain_query
        mean = jnp.mean(weighted * wide, axis=-1, keepdims=True)
        og_ref[g >> 1, 1, g & 1] = (scale * weighted - wide * (scale * scale * scale) * mean).astype(jnp.bfloat16)

    start = 0
    for which, most in enumerate(BUCKETS):
        stop = (stops[which] + TOGETHER - 1) // TOGETHER

        @pl.loop(start, stop)
        def _(step, most=most):
            states = [forward(step * TOGETHER + u, most, u == 0) for u in range(TOGETHER)]
            for state in states:
                backward(state, most)

        start = stop

    back = [pltpu.make_async_copy(og_ref, og_hbm, out_sems.at[8])]
    back[0].start()
    for i in SEND_ORDER:

        @pl.loop(i * 16, i * 16 + 16, unroll=2)
        def _(t, i=i):
            both = acc[t]
            k = (both[:, :128] * INV_ROOT).astype(jnp.bfloat16)
            stage[i, 0, t - i * 16] = k
            stage[i, 1, t - i * 16] = both[:, 128:].astype(jnp.bfloat16)
            sums = jnp.sum(k.astype(jnp.float32) * ktab[t].astype(jnp.float32), axis=0, keepdims=True)
            gain_key_ref[0:1, :] += sums

        back.append(pltpu.make_async_copy(stage.at[i], parts[i], out_sems.at[i]))
        back[-1].start()
    gain_key_ref[0:1, :] = gain_key_ref[0:1, :] / gain_key
    for copy in back:
        copy.wait()


def attend(info, counts, lists, pieces, qg, query_gain, key_gain):
    smem = pl.BlockSpec(memory_space=pltpu.SMEM)
    vmem = pl.BlockSpec(memory_space=pltpu.VMEM)
    hbm = pl.BlockSpec(memory_space=pl.ANY)
    part = jax.ShapeDtypeStruct((2, 16, 128, 128), jnp.bfloat16)
    row = jax.ShapeDtypeStruct((8, 128), jnp.float32)
    return pl.pallas_call(
        attend_kernel,
        out_shape=(jax.ShapeDtypeStruct((16, 2, 2, 128, 128), jnp.bfloat16),) + (part,) * 8 + (row, row),
        in_specs=[smem] * 3 + [hbm] * 9 + [vmem] * 2,
        out_specs=(hbm,) * 9 + (vmem,) * 2,
        scratch_shapes=[
            pltpu.VMEM((128, 128, 128), jnp.bfloat16),
            pltpu.VMEM((128, 128, 128), jnp.bfloat16),
            pltpu.VMEM((128, 128, 256), jnp.float32),
            pltpu.VMEM((16, 2, 2, 128, 128), jnp.bfloat16),
            pltpu.VMEM((16, 2, 2, 128, 128), jnp.bfloat16),
            pltpu.VMEM((8, 2, 16, 128, 128), jnp.bfloat16),
            pltpu.SMEM((GROUPS,), jnp.int32),
            pltpu.SemaphoreType.DMA((17,)),
            pltpu.SemaphoreType.DMA((9,)),
        ],
        compiler_params=pltpu.CompilerParams(vmem_limit_bytes=56 * 1024 * 1024),
        cost_estimate=pl.CostEstimate(flops=6 * 10**9, bytes_accessed=20 * 2**20, transcendentals=4 * 2**20),
        name="attend",
    )(info, counts, lists, *pieces, qg, query_gain, key_gain)


HEADS = 16
ALONG_Z = [[8 * z + rest for z in range(8)] for rest in range(8)]
ROWS = jax.ShapeDtypeStruct((256, HEADS * HEAD_DIM), jnp.bfloat16)
PAIRS = jax.ShapeDtypeStruct((8, 2, 2, 256, HEAD_DIM), jnp.bfloat16)
HALF_PAIRS = jax.ShapeDtypeStruct((8, 2, 256, HEAD_DIM), jnp.bfloat16)


def columns(head):
    if isinstance(head, int):
        return pl.ds(head * HEAD_DIM, HEAD_DIM)
    return pl.ds(pl.multiple_of(head * HEAD_DIM, HEAD_DIM), HEAD_DIM)


def staged(groups, in_sems, out_sems):
    loads, stores = [], []
    for ins, _ in groups:
        made = [pltpu.make_async_copy(a, b, in_sems.at[sum(map(len, loads)) + i]) for i, (a, b) in enumerate(ins)]
        loads.append(made)
    for made in loads:
        for copy in made:
            copy.start()
    for made, (_, outs) in zip(loads, groups):
        for copy in made:
            copy.wait()
        for a, b in outs:
            stores.append(pltpu.make_async_copy(a, b, out_sems.at[len(stores)]))
            stores[-1].start()
    for copy in stores:
        copy.wait()


def pack_kernel(a_ref, b_ref, out_ref, buf, in_sems, out_sems):
    staged([([(ref.at[:, columns(2 * z + hh)], buf.at[z, hh, i])
              for hh in range(2) for i, ref in enumerate((a_ref, b_ref))], [(buf.at[z], out_ref.at[z])])
            for z in range(8)], in_sems, out_sems)


def give_kernel(mine_ref, a_ref, b_ref, out_ref, buf, in_sems, out_sems):
    staged([([(ref.at[:, columns(2 * z + 1 - mine_ref[0])], buf.at[z, i]) for i, ref in enumerate((a_ref, b_ref))],
             [(buf.at[z], out_ref.at[z])]) for z in range(8)], in_sems, out_sems)


def pack_pair_kernel(mine_ref, a_ref, b_ref, got_ref, out_ref, buf, in_sems, out_sems):
    staged([([(got_ref.at[z], buf.at[z, 1])]
             + [(ref.at[:, columns(2 * z + mine_ref[0])], buf.at[z, 0, i]) for i, ref in enumerate((a_ref, b_ref))],
             [(buf.at[z], out_ref.at[z])]) for z in range(8)], in_sems, out_sems)


def plane_columns(z):
    return pl.ds(z * 2 * HEAD_DIM, 2 * HEAD_DIM)


def unpack_kernel(in_ref, a_ref, b_ref, buf, in_sems, out_sems):
    staged([([(in_ref.at[z, hh, i], buf.at[i, :, columns(2 * z + hh)]) for hh in range(2) for i in range(2)],
             [(buf.at[i, :, plane_columns(z)], ref.at[:, plane_columns(z)]) for i, ref in enumerate((a_ref, b_ref))])
            for z in range(8)], in_sems, out_sems)


def unpack_front_kernel(mine_ref, in_ref, got_ref, a_ref, b_ref, buf, in_sems, out_sems):
    half = mine_ref[0]
    staged([([(in_ref.at[z, 0, i], buf.at[i, :, columns(2 * z + half)]) for i in range(2)]
             + [(got_ref.at[z, i], buf.at[i, :, columns(2 * z + 1 - half)]) for i in range(2)],
             [(buf.at[i, :, plane_columns(z)], ref.at[:, plane_columns(z)]) for i, ref in enumerate((a_ref, b_ref))])
            for z in range(8)], in_sems, out_sems)


def mover(kernel, name, out_shape, *args):
    smem = pl.BlockSpec(memory_space=pltpu.SMEM)
    hbm = pl.BlockSpec(memory_space=pl.ANY)
    many = isinstance(out_shape, tuple)
    return pl.pallas_call(
        kernel,
        out_shape=out_shape,
        in_specs=[smem if a.dtype == jnp.int32 else hbm for a in args],
        out_specs=(hbm,) * len(out_shape) if many else hbm,
        scratch_shapes=[
            pltpu.VMEM((2,) + ROWS.shape if many else out_shape.shape, jnp.bfloat16),
            pltpu.SemaphoreType.DMA((32,)),
            pltpu.SemaphoreType.DMA((16,)),
        ],
        compiler_params=pltpu.CompilerParams(vmem_limit_bytes=24 * 1024 * 1024),
        cost_estimate=pl.CostEstimate(flops=0, bytes_accessed=2**22, transcendentals=0),
        name=name,
    )(*args)


def norm_kernel(mine_ref, kv_hbm, gain_ref, own_hbm, cross_hbm, kv, out, in_sems, out_sems):
    half = mine_ref[0]
    plane = mine_ref[1]
    loads = [pltpu.make_async_copy(kv_hbm.at[z], kv.at[z], in_sems.at[z]) for z in range(8)]
    for load in loads:
        load.start()
    stores = []
    for z in range(8):
        loads[z].wait()
        for which, target in ((0, cross_hbm), (1, own_hbm)):
            hh = half if which else 1 - half
            wide = kv[z, hh, 0].astype(jnp.float32)
            scale = lax.rsqrt(jnp.mean(wide * wide, axis=-1, keepdims=True) + EPS)
            out[which, z] = (wide * scale * gain_ref[pl.ds(2 * plane + hh, 1), :]).astype(jnp.bfloat16)
            stores.append(pltpu.make_async_copy(out.at[which, z], target.at[0, z], out_sems.at[4 * z + 2 * which]))
            stores.append(pltpu.make_async_copy(kv.at[z, hh, 1], target.at[1, z], out_sems.at[4 * z + 2 * which + 1]))
            stores[-2].start()
            stores[-1].start()
    for store in stores:
        store.wait()


def norm(mine, kv, gain):
    hbm = pl.BlockSpec(memory_space=pl.ANY)
    piece = jax.ShapeDtypeStruct((2, 8, 256, HEAD_DIM), jnp.bfloat16)
    return pl.pallas_call(
        norm_kernel,
        out_shape=(piece, piece),
        in_specs=[pl.BlockSpec(memory_space=pltpu.SMEM), hbm, pl.BlockSpec(memory_space=pltpu.VMEM)],
        out_specs=(hbm, hbm),
        scratch_shapes=[
            pltpu.VMEM((8, 2, 2, 256, HEAD_DIM), jnp.bfloat16),
            pltpu.VMEM((2, 8, 256, HEAD_DIM), jnp.bfloat16),
            pltpu.SemaphoreType.DMA((8,)),
            pltpu.SemaphoreType.DMA((32,)),
        ],
        compiler_params=pltpu.CompilerParams(vmem_limit_bytes=24 * 1024 * 1024),
        cost_estimate=pl.CostEstimate(flops=10**7, bytes_accessed=2**22, transcendentals=2**13),
        name="norm",
    )(mine, kv, gain)


def finish_kernel(mine_ref, part_hbm, core_hbm, side_hbm, far_hbm, kv_hbm, gain_ref, out_hbm,
                  sums, kv, out, in_sems, out_sems):
    half = mine_ref[0]
    plane = mine_ref[1]
    loads = []
    for z in range(8):
        for i, ref in enumerate((part_hbm, core_hbm, side_hbm, far_hbm)):
            loads.append(pltpu.make_async_copy(ref.at[:, z], sums.at[i, :, z], in_sems.at[5 * z + i]))
        loads.append(pltpu.make_async_copy(kv_hbm.at[z, :, 0], kv.at[z], in_sems.at[5 * z + 4]))
    for load in loads:
        load.start()
    stores = []
    for z in range(8):
        for load in loads[5 * z:5 * z + 5]:
            load.wait()
        for own in (True, False):
            hh = half if own else 1 - half
            gain = gain_ref[pl.ds(2 * plane + hh, 1), :]
            if own:
                total = [functools.reduce(jnp.add, [sums[j, i, z].astype(jnp.float32) for j in range(3)]) for i in range(2)]
            else:
                total = [sums[3, i, z].astype(jnp.float32) for i in range(2)]
            wide = kv[z, hh].astype(jnp.float32)
            scale = lax.rsqrt(jnp.mean(wide * wide, axis=-1, keepdims=True) + EPS)
            weighted = total[0] * gain
            inner = jnp.mean(weighted * wide, axis=-1, keepdims=True)
            out[z, hh, 0] = (scale * weighted - wide * (scale * scale * scale) * inner).astype(jnp.bfloat16)
            out[z, hh, 1] = total[1].astype(jnp.bfloat16)
        stores.append(pltpu.make_async_copy(out.at[z], out_hbm.at[z], out_sems.at[z]))
        stores[-1].start()
    for store in stores:
        store.wait()


def finish(mine, part, core, side, far, kv, gain):
    hbm = pl.BlockSpec(memory_space=pl.ANY)
    return pl.pallas_call(
        finish_kernel,
        out_shape=PAIRS,
        in_specs=[pl.BlockSpec(memory_space=pltpu.SMEM)] + [hbm] * 5 + [pl.BlockSpec(memory_space=pltpu.VMEM)],
        out_specs=hbm,
        scratch_shapes=[
            pltpu.VMEM((4, 2, 8, 256, HEAD_DIM), jnp.bfloat16),
            pltpu.VMEM((8, 2, 256, HEAD_DIM), jnp.bfloat16),
            pltpu.VMEM((8, 2, 2, 256, HEAD_DIM), jnp.bfloat16),
            pltpu.SemaphoreType.DMA((40,)),
            pltpu.SemaphoreType.DMA((8,)),
        ],
        compiler_params=pltpu.CompilerParams(vmem_limit_bytes=24 * 1024 * 1024),
        cost_estimate=pl.CostEstimate(flops=10**7, bytes_accessed=2**23, transcendentals=2**13),
        name="finish",
    )(mine, part, core, side, far, kv, gain)


def along_z(array):
    return lax.all_to_all(array, "seq", split_axis=0, concat_axis=0, axis_index_groups=ALONG_Z, tiled=True)


def across(array, flip):
    return lax.ppermute(array, "seq", [(i, i ^ flip) for i in range(64)])


def wide_sum(*arrays):
    return functools.reduce(jnp.add, [a.astype(jnp.float32) for a in arrays]).astype(jnp.bfloat16)


def over_copies(row):
    for flip in (1, 2):
        row = row + lax.ppermute(row, "dp", [(i, i ^ flip) for i in range(4)])
    for flip in (1, 2):
        row = row + across(row, flip)
    return row


def body(query_rows, key_rows, value_rows, output_grad, query_gain, key_gain, block_list, block_count):
    position = lax.axis_index("seq")
    head = position // 4
    plane = position // 8
    half = head % 2
    lists = lax.dynamic_slice_in_dim(block_list[0], head, 1, 0).reshape(1024)
    counts = lax.dynamic_slice_in_dim(block_count[0], head, 1, 0).reshape(128)
    info = jnp.stack([position % 8, head]).astype(jnp.int32)
    mine = jnp.stack([half, plane]).astype(jnp.int32)

    with jax.named_scope("gather"):
        kv = along_z(mover(pack_kernel, "pack", PAIRS, key_rows[0], value_rows[0]))
        got = across(mover(give_kernel, "give", HALF_PAIRS, mine, query_rows[0], output_grad[0]), 6)
        pair_send = mover(pack_pair_kernel, "pack_pair", PAIRS, mine, query_rows[0], output_grad[0], got)
        pair_send, kv, lists, counts, info = lax.optimization_barrier((pair_send, kv, lists, counts, info))
        own, cross_send = norm(mine, kv, key_gain)
        cross = across(cross_send, 6)
        side = across(own, 2)
        query_pair = along_z(pair_send)
        far = across(cross, 2)
        pieces = []
        for piece in (own, side, far, cross):
            pieces += [piece, across(piece, 1)]
        pieces = [p.reshape(2, 16, 128, 128) for p in pieces]
    with jax.named_scope("attend"):
        outs = attend(info, counts, lists, pieces, query_pair.reshape(16, 2, 2, 128, 128), query_gain, key_gain)
    front, parts, query_row, key_row = outs[0], outs[1:9], outs[9], outs[10]
    with jax.named_scope("return"):
        far = wide_sum(parts[4], across(parts[5], 1))
        side = wide_sum(parts[2], across(parts[3], 1))
        far = across(far, 2)
        front, side = lax.optimization_barrier((front, side))
        front = along_z(front.reshape(8, 2, 2, 256, HEAD_DIM))
        side = across(side, 2)
        cross = across(wide_sum(parts[6], across(parts[7], 1), far), 6)
        core = across(parts[1], 1)
        shape = (2, 8, 256, HEAD_DIM)
        kv_grad = finish(mine, parts[0].reshape(shape), core.reshape(shape), side.reshape(shape), cross.reshape(shape), kv, key_gain)
    with jax.named_scope("gains"):
        rows = over_copies(jnp.concatenate([query_row[0:1], key_row[0:1]]))
        other = across(rows, 4)
        rows = jnp.where(half == 0, jnp.stack([rows, other]), jnp.stack([other, rows]))
        rows, kv_grad = lax.optimization_barrier((rows, kv_grad))
        index = jnp.arange(8, dtype=jnp.int32)[:, None, None, None]
        table = jnp.where(index == plane, rows[None], 0.0)
        for d in range(1, 8):
            came = lax.ppermute(rows, "seq", [(i, (i + 8 * d) % 64) for i in range(64)])
            table = jnp.where(index == (plane - d) % 8, came[None], table)
        table = table.reshape(HEADS, 2, HEAD_DIM)
    with jax.named_scope("return"):
        got = across(front[:, 1], 6)
        attended, query_grad = mover(unpack_front_kernel, "unpack_front", (ROWS, ROWS), mine, front, got)
        key_grad, value_grad = mover(unpack_kernel, "unpack", (ROWS, ROWS), along_z(kv_grad))
    return (attended[None], query_grad[None], key_grad[None], value_grad[None], table[:, 0], table[:, 1])


def solution(mesh):
    rows = P("dp", "seq", None)
    return jax.shard_map(
        body,
        mesh=mesh,
        in_specs=(rows, rows, rows, rows, P(), P(), P("dp", None, None, None), P("dp", None, None)),
        out_specs=(rows, rows, rows, rows, P(), P()),
        check_vma=False,
    )
```

```python
import functools
import math

import jax
import jax.numpy as jnp
from jax import lax
from jax.experimental import pallas as pl
from jax.experimental.pallas import tpu as pltpu
from jax.sharding import PartitionSpec as P

HEAD_DIM = 128
EPS = 1e-06
INV_ROOT = 1.0 / math.sqrt(HEAD_DIM)
LOG2E = math.log2(math.e)
NT = (((1,), (1,)), ((), ()))
TN = (((0,), (0,)), ((), ()))
NN = (((1,), (0,)), ((), ()))
GROUPS = 32
BUCKETS = (8, 6, 4, 2)
TOGETHER = 1
SEND_ORDER = (5, 3, 1, 7, 4, 2, 0, 6)


def dot(a, b, dims):
    return lax.dot_general(a, b, dims, preferred_element_type=jnp.float32)


def attend_kernel(info_ref, count_ref, list_ref, *refs):
    pieces = refs[:8]
    qg_hbm, query_gain_ref, key_gain_ref, og_hbm = refs[8:12]
    parts = refs[12:20]
    gain_query_ref, gain_key_ref, ktab, vtab, acc, qg_ref, og_ref, stage, order_ref, in_sems, out_sems = refs[20:]
    place_x_core = info_ref[0]
    head = info_ref[1]
    copies = [pltpu.make_async_copy(qg_hbm, qg_ref, in_sems.at[16])]
    for i, piece in enumerate(pieces):
        for j, table in enumerate((ktab, vtab)):
            copies.append(pltpu.make_async_copy(piece.at[j], table.at[pl.ds(i * 16, 16)], in_sems.at[2 * i + j]))
    for copy in copies:
        copy.start()

    def block_of(g):
        across = place_x_core ^ (6 * ((g >> 1) & 1))
        return (g >> 2) * 16 + across * 2 + (g & 1)

    stops = []
    stop = 0
    for which, most in enumerate(BUCKETS):
        below = BUCKETS[which + 1] if which + 1 < len(BUCKETS) else 0

        def place(g, at, most=most, below=below):
            count = count_ref[block_of(g)]
            inside = jnp.logical_and(count <= most, count > below)

            @pl.when(inside)
            def _():
                order_ref[at] = g

            return at + inside.astype(jnp.int32)

        stop = lax.fori_loop(0, GROUPS, place, jnp.int32(stop))
        stops.append(stop)

    @pl.loop(0, 128)
    def _(t):
        acc[t] = jnp.zeros((128, 256), jnp.float32)

    gain_query = query_gain_ref[pl.ds(head, 1), :]
    gain_key = key_gain_ref[pl.ds(head, 1), :]
    gain_query_ref[...] = jnp.zeros_like(gain_query_ref)
    gain_key_ref[...] = jnp.zeros_like(gain_key_ref)
    for copy in copies:
        copy.wait()

    zero = jnp.zeros((128, 128), jnp.bfloat16)

    def forward(i, most, first):
        g = order_ref[i]
        block = block_of(g)
        live = count_ref[block]
        listed = [list_ref[block * 8 + j] for j in range(most)]
        spots = [(((c >> 1) & 7) ^ place_x_core) * 16 + (c >> 4) * 2 + (c & 1) for c in listed]
        wide = qg_ref[g >> 1, 0, g & 1].astype(jnp.float32)
        grad = qg_ref[g >> 1, 1, g & 1]
        scale = lax.rsqrt(jnp.mean(wide * wide, axis=-1, keepdims=True) + EPS)
        hat = wide * scale
        normed = (hat * gain_query).astype(jnp.bfloat16)
        keys = jnp.concatenate([ktab[t] for t in spots], axis=0)
        values = jnp.concatenate([vtab[t] for t in spots], axis=0)
        flat = dot(normed, keys, NT)
        scores = []
        for j in range(most):
            s = flat[:, j * 128:(j + 1) * 128]
            if j == most - 1 or (j and not first):
                s = jnp.where(j < live, s, -jnp.inf)
            scores.append(s)
        top = jnp.max(functools.reduce(jnp.maximum, scores), axis=-1, keepdims=True)
        exps = [jnp.exp2((s - top) * (INV_ROOT * LOG2E)) for s in scores]
        total = jnp.sum(functools.reduce(jnp.add, exps), axis=-1, keepdims=True)
        inverse = 1.0 / total
        weights = [(e * inverse).astype(jnp.bfloat16) for e in exps]
        attended = dot(jnp.concatenate(weights, axis=1), values, NN).astype(jnp.bfloat16)
        row = pl.multiple_of(((g >> 1) & 1) * 512 + (g & 1) * 128, 128)
        og_ref[g >> 2, pl.ds(row, 128)] = attended
        inner = jnp.sum(grad.astype(jnp.float32) * attended.astype(jnp.float32), axis=-1, keepdims=True)
        return g, spots, wide, grad, scale, hat, normed, keys, values, weights, inner

    def backward(state, most):
        g, spots, wide, grad, scale, hat, normed, keys, values, weights, inner = state
        flat = dot(grad, values, NT)
        score_grads = []
        for j in range(most):
            wg = flat[:, j * 128:(j + 1) * 128]
            score_grads.append((weights[j].astype(jnp.float32) * (wg - inner)).astype(jnp.bfloat16))
        norm_grad = dot(jnp.concatenate(score_grads, axis=1), keys, NN) * INV_ROOT
        pair = jnp.concatenate(
            [jnp.concatenate([normed, zero], axis=1), jnp.concatenate([zero, grad], axis=1)], axis=0
        )
        for j in range(most):
            acc[spots[j]] += dot(jnp.concatenate([score_grads[j], weights[j]], axis=0), pair, TN)
        gain_query_ref[0:1, :] += jnp.sum(norm_grad * hat, axis=0, keepdims=True)
        weighted = norm_grad * gain_query
        mean = jnp.mean(weighted * wide, axis=-1, keepdims=True)
        row = pl.multiple_of(((g >> 1) & 1) * 512 + (g & 1) * 128 + 256, 128)
        og_ref[g >> 2, pl.ds(row, 128)] = (scale * weighted - wide * (scale * scale * scale) * mean).astype(jnp.bfloat16)

    start = 0
    for which, most in enumerate(BUCKETS):
        stop = (stops[which] + TOGETHER - 1) // TOGETHER

        @pl.loop(start, stop)
        def _(step, most=most):
            states = [forward(step * TOGETHER + u, most, u == 0) for u in range(TOGETHER)]
            for state in states:
                backward(state, most)

        start = stop

    rows = pl.ds(0, 1024)
    back = [pltpu.make_async_copy(og_ref.at[:, rows], og_hbm.at[:, rows], out_sems.at[8])]
    back[0].start()
    for i in SEND_ORDER:

        @pl.loop(i * 16, i * 16 + 16, unroll=2)
        def _(t, i=i):
            both = acc[t]
            k = (both[:, :128] * INV_ROOT).astype(jnp.bfloat16)
            stage[i, 0, t - i * 16] = k
            stage[i, 1, t - i * 16] = both[:, 128:].astype(jnp.bfloat16)
            sums = jnp.sum(k.astype(jnp.float32) * ktab[t].astype(jnp.float32), axis=0, keepdims=True)
            gain_key_ref[0:1, :] += sums

        back.append(pltpu.make_async_copy(stage.at[i], parts[i], out_sems.at[i]))
        back[-1].start()
    split = []
    for wide in (gain_query_ref[0:1, :], gain_key_ref[0:1, :] / gain_key):
        for _ in range(3):
            split.append(wide.astype(jnp.bfloat16).astype(jnp.float32))
            wide = wide - split[-1]
    split = jnp.concatenate(split + [jnp.zeros((10, 128), jnp.float32)], axis=0).astype(jnp.bfloat16)
    for z in range(8):
        og_ref[z, 1024:1040] = split
    rows = pl.ds(1024, 16)
    back.append(pltpu.make_async_copy(og_ref.at[:, rows], og_hbm.at[:, rows], out_sems.at[9]))
    back[-1].start()
    for copy in back:
        copy.wait()


def attend(info, counts, lists, pieces, qg, query_gain, key_gain):
    smem = pl.BlockSpec(memory_space=pltpu.SMEM)
    vmem = pl.BlockSpec(memory_space=pltpu.VMEM)
    hbm = pl.BlockSpec(memory_space=pl.ANY)
    part = jax.ShapeDtypeStruct((2, 16, 128, 128), jnp.bfloat16)
    return pl.pallas_call(
        attend_kernel,
        out_shape=(jax.ShapeDtypeStruct((8, 1040, 128), jnp.bfloat16),) + (part,) * 8,
        in_specs=[smem] * 3 + [hbm] * 9 + [vmem] * 2,
        out_specs=(hbm,) * 9,
        scratch_shapes=[
            pltpu.VMEM((8, 128), jnp.float32),
            pltpu.VMEM((8, 128), jnp.float32),
            pltpu.VMEM((128, 128, 128), jnp.bfloat16),
            pltpu.VMEM((128, 128, 128), jnp.bfloat16),
            pltpu.VMEM((128, 128, 256), jnp.float32),
            pltpu.VMEM((16, 2, 2, 128, 128), jnp.bfloat16),
            pltpu.VMEM((8, 1040, 128), jnp.bfloat16),
            pltpu.VMEM((8, 2, 16, 128, 128), jnp.bfloat16),
            pltpu.SMEM((GROUPS,), jnp.int32),
            pltpu.SemaphoreType.DMA((17,)),
            pltpu.SemaphoreType.DMA((10,)),
        ],
        compiler_params=pltpu.CompilerParams(vmem_limit_bytes=56 * 1024 * 1024),
        cost_estimate=pl.CostEstimate(flops=6 * 10**9, bytes_accessed=20 * 2**20, transcendentals=4 * 2**20),
        name="attend",
    )(info, counts, lists, *pieces, qg, query_gain, key_gain)


HEADS = 16
ALONG_Z = [[8 * z + rest for z in range(8)] for rest in range(8)]
ROWS = jax.ShapeDtypeStruct((256, HEADS * HEAD_DIM), jnp.bfloat16)
PAIRS = jax.ShapeDtypeStruct((8, 2, 2, 256, HEAD_DIM), jnp.bfloat16)
HALF_PAIRS = jax.ShapeDtypeStruct((8, 2, 256, HEAD_DIM), jnp.bfloat16)


def columns(head):
    if isinstance(head, int):
        return pl.ds(head * HEAD_DIM, HEAD_DIM)
    return pl.ds(pl.multiple_of(head * HEAD_DIM, HEAD_DIM), HEAD_DIM)


def staged(groups, in_sems, out_sems):
    loads, stores = [], []
    for ins, _ in groups:
        made = [pltpu.make_async_copy(a, b, in_sems.at[sum(map(len, loads)) + i]) for i, (a, b) in enumerate(ins)]
        loads.append(made)
    for made in loads:
        for copy in made:
            copy.start()
    for made, (_, outs) in zip(loads, groups):
        for copy in made:
            copy.wait()
        for a, b in outs:
            stores.append(pltpu.make_async_copy(a, b, out_sems.at[len(stores)]))
            stores[-1].start()
    for copy in stores:
        copy.wait()


def pack_kernel(a_ref, b_ref, out_ref, buf, in_sems, out_sems):
    staged([([(ref.at[:, columns(2 * z + hh)], buf.at[z, hh, i])
              for hh in range(2) for i, ref in enumerate((a_ref, b_ref))], [(buf.at[z], out_ref.at[z])])
            for z in range(8)], in_sems, out_sems)


def give_kernel(mine_ref, a_ref, b_ref, out_ref, buf, in_sems, out_sems):
    staged([([(ref.at[:, columns(2 * z + 1 - mine_ref[0])], buf.at[z, i]) for i, ref in enumerate((a_ref, b_ref))],
             [(buf.at[z], out_ref.at[z])]) for z in range(8)], in_sems, out_sems)


def pack_pair_kernel(mine_ref, a_ref, b_ref, got_ref, out_ref, buf, in_sems, out_sems):
    staged([([(got_ref.at[z], buf.at[z, 1])]
             + [(ref.at[:, columns(2 * z + mine_ref[0])], buf.at[z, 0, i]) for i, ref in enumerate((a_ref, b_ref))],
             [(buf.at[z], out_ref.at[z])]) for z in range(8)], in_sems, out_sems)


def plane_columns(z):
    return pl.ds(z * 2 * HEAD_DIM, 2 * HEAD_DIM)


def unpack_kernel(in_ref, a_ref, b_ref, buf, in_sems, out_sems):
    staged([([(in_ref.at[z, hh, i], buf.at[i, :, columns(2 * z + hh)]) for hh in range(2) for i in range(2)],
             [(buf.at[i, :, plane_columns(z)], ref.at[:, plane_columns(z)]) for i, ref in enumerate((a_ref, b_ref))])
            for z in range(8)], in_sems, out_sems)


def unpack_front_kernel(mine_ref, in_ref, got_ref, a_ref, b_ref, buf, in_sems, out_sems):
    half = mine_ref[0]
    staged([([(in_ref.at[z, pl.ds(i * 256, 256)], buf.at[i, :, columns(2 * z + half)]) for i in range(2)]
             + [(got_ref.at[z, pl.ds(i * 256, 256)], buf.at[i, :, columns(2 * z + 1 - half)]) for i in range(2)],
             [(buf.at[i, :, plane_columns(z)], ref.at[:, plane_columns(z)]) for i, ref in enumerate((a_ref, b_ref))])
            for z in range(8)], in_sems, out_sems)


def mover(kernel, name, out_shape, *args):
    smem = pl.BlockSpec(memory_space=pltpu.SMEM)
    hbm = pl.BlockSpec(memory_space=pl.ANY)
    many = isinstance(out_shape, tuple)
    return pl.pallas_call(
        kernel,
        out_shape=out_shape,
        in_specs=[smem if a.dtype == jnp.int32 else hbm for a in args],
        out_specs=(hbm,) * len(out_shape) if many else hbm,
        scratch_shapes=[
            pltpu.VMEM((2,) + ROWS.shape if many else out_shape.shape, jnp.bfloat16),
            pltpu.SemaphoreType.DMA((32,)),
            pltpu.SemaphoreType.DMA((16,)),
        ],
        compiler_params=pltpu.CompilerParams(vmem_limit_bytes=56 * 1024 * 1024),
        cost_estimate=pl.CostEstimate(flops=0, bytes_accessed=2**22, transcendentals=0),
        name=name,
    )(*args)


def norm_kernel(mine_ref, kv_hbm, gain_ref, own_hbm, cross_hbm, kv, out, in_sems, out_sems):
    half = mine_ref[0]
    plane = mine_ref[1]
    loads = [pltpu.make_async_copy(kv_hbm.at[z], kv.at[z], in_sems.at[z]) for z in range(8)]
    for load in loads:
        load.start()
    stores = []
    for z in range(8):
        loads[z].wait()
        for which, target in ((0, cross_hbm), (1, own_hbm)):
            hh = half if which else 1 - half
            wide = kv[z, hh, 0].astype(jnp.float32)
            scale = lax.rsqrt(jnp.mean(wide * wide, axis=-1, keepdims=True) + EPS)
            out[which, z] = (wide * scale * gain_ref[pl.ds(2 * plane + hh, 1), :]).astype(jnp.bfloat16)
            stores.append(pltpu.make_async_copy(out.at[which, z], target.at[0, z], out_sems.at[4 * z + 2 * which]))
            stores.append(pltpu.make_async_copy(kv.at[z, hh, 1], target.at[1, z], out_sems.at[4 * z + 2 * which + 1]))
            stores[-2].start()
            stores[-1].start()
    for store in stores:
        store.wait()


def norm(mine, kv, gain):
    hbm = pl.BlockSpec(memory_space=pl.ANY)
    piece = jax.ShapeDtypeStruct((2, 8, 256, HEAD_DIM), jnp.bfloat16)
    return pl.pallas_call(
        norm_kernel,
        out_shape=(piece, piece),
        in_specs=[pl.BlockSpec(memory_space=pltpu.SMEM), hbm, pl.BlockSpec(memory_space=pltpu.VMEM)],
        out_specs=(hbm, hbm),
        scratch_shapes=[
            pltpu.VMEM((8, 2, 2, 256, HEAD_DIM), jnp.bfloat16),
            pltpu.VMEM((2, 8, 256, HEAD_DIM), jnp.bfloat16),
            pltpu.SemaphoreType.DMA((8,)),
            pltpu.SemaphoreType.DMA((32,)),
        ],
        compiler_params=pltpu.CompilerParams(vmem_limit_bytes=56 * 1024 * 1024),
        cost_estimate=pl.CostEstimate(flops=10**7, bytes_accessed=2**22, transcendentals=2**13),
        name="norm",
    )(mine, kv, gain)


def finish_kernel(mine_ref, part_hbm, core_hbm, side_hbm, far_hbm, kv_hbm, gain_ref, out_hbm,
                  sums, kv, out, in_sems, out_sems):
    half = mine_ref[0]
    plane = mine_ref[1]
    loads = []
    for z in range(8):
        for i, ref in enumerate((part_hbm, core_hbm, side_hbm, far_hbm)):
            loads.append(pltpu.make_async_copy(ref.at[:, z], sums.at[i, :, z], in_sems.at[5 * z + i]))
        loads.append(pltpu.make_async_copy(kv_hbm.at[z, :, 0], kv.at[z], in_sems.at[5 * z + 4]))
    for load in loads:
        load.start()
    stores = []
    for z in range(8):
        for load in loads[5 * z:5 * z + 5]:
            load.wait()
        for own in (True, False):
            hh = half if own else 1 - half
            gain = gain_ref[pl.ds(2 * plane + hh, 1), :]
            if own:
                total = [functools.reduce(jnp.add, [sums[j, i, z].astype(jnp.float32) for j in range(3)]) for i in range(2)]
            else:
                total = [sums[3, i, z].astype(jnp.float32) for i in range(2)]
            wide = kv[z, hh].astype(jnp.float32)
            scale = lax.rsqrt(jnp.mean(wide * wide, axis=-1, keepdims=True) + EPS)
            weighted = total[0] * gain
            inner = jnp.mean(weighted * wide, axis=-1, keepdims=True)
            out[z, hh, 0] = (scale * weighted - wide * (scale * scale * scale) * inner).astype(jnp.bfloat16)
            out[z, hh, 1] = total[1].astype(jnp.bfloat16)
        stores.append(pltpu.make_async_copy(out.at[z], out_hbm.at[z], out_sems.at[z]))
        stores[-1].start()
    for store in stores:
        store.wait()


def finish(mine, part, core, side, far, kv, gain):
    hbm = pl.BlockSpec(memory_space=pl.ANY)
    return pl.pallas_call(
        finish_kernel,
        out_shape=PAIRS,
        in_specs=[pl.BlockSpec(memory_space=pltpu.SMEM)] + [hbm] * 5 + [pl.BlockSpec(memory_space=pltpu.VMEM)],
        out_specs=hbm,
        scratch_shapes=[
            pltpu.VMEM((4, 2, 8, 256, HEAD_DIM), jnp.bfloat16),
            pltpu.VMEM((8, 2, 256, HEAD_DIM), jnp.bfloat16),
            pltpu.VMEM((8, 2, 2, 256, HEAD_DIM), jnp.bfloat16),
            pltpu.SemaphoreType.DMA((40,)),
            pltpu.SemaphoreType.DMA((8,)),
        ],
        compiler_params=pltpu.CompilerParams(vmem_limit_bytes=56 * 1024 * 1024),
        cost_estimate=pl.CostEstimate(flops=10**7, bytes_accessed=2**23, transcendentals=2**13),
        name="finish",
    )(mine, part, core, side, far, kv, gain)


def along_z(array):
    return lax.all_to_all(array, "seq", split_axis=0, concat_axis=0, axis_index_groups=ALONG_Z, tiled=True)


def across(array, flip):
    return lax.ppermute(array, "seq", [(i, i ^ flip) for i in range(64)])


def wide_sum(*arrays):
    return functools.reduce(jnp.add, [a.astype(jnp.float32) for a in arrays]).astype(jnp.bfloat16)


def over_four(array, axis, step):
    size = lax.axis_size(axis)
    one, two, three = [lax.ppermute(array, axis, [(i, i ^ (step * f)) for i in range(size)]) for f in (1, 2, 3)]
    return (array + one) + (two + three)


def body(query_rows, key_rows, value_rows, output_grad, query_gain, key_gain, block_list, block_count):
    position = lax.axis_index("seq")
    head = position // 4
    plane = position // 8
    half = head % 2
    lists = lax.dynamic_slice_in_dim(block_list[0], head, 1, 0).reshape(1024)
    counts = lax.dynamic_slice_in_dim(block_count[0], head, 1, 0).reshape(128)
    info = jnp.stack([position % 8, head]).astype(jnp.int32)
    mine = jnp.stack([half, plane]).astype(jnp.int32)

    with jax.named_scope("gather"):
        kv = along_z(mover(pack_kernel, "pack", PAIRS, key_rows[0], value_rows[0]))
        got = across(mover(give_kernel, "give", HALF_PAIRS, mine, query_rows[0], output_grad[0]), 6)
        pair_send = mover(pack_pair_kernel, "pack_pair", PAIRS, mine, query_rows[0], output_grad[0], got)
        pair_send, kv, lists, counts, info = lax.optimization_barrier((pair_send, kv, lists, counts, info))
        own, cross_send = norm(mine, kv, key_gain)
        cross = across(cross_send, 6)
        side = across(own, 2)
        query_pair = along_z(pair_send)
        far = across(cross, 2)
        pieces = []
        for piece in (own, side, far, cross):
            pieces += [piece, across(piece, 1)]
        pieces = [p.reshape(2, 16, 128, 128) for p in pieces]
    with jax.named_scope("attend"):
        outs = attend(info, counts, lists, pieces, query_pair.reshape(16, 2, 2, 128, 128), query_gain, key_gain)
    front, parts = outs[0], outs[1:9]
    with jax.named_scope("return"):
        far = wide_sum(parts[4], across(parts[5], 1))
        side = wide_sum(parts[2], across(parts[3], 1))
        far = across(far, 2)
        front, side = lax.optimization_barrier((front, side))
        front = along_z(front)
        far, side = lax.optimization_barrier((far, side))
        side = across(side, 2)
        cross = across(wide_sum(parts[6], across(parts[7], 1), far), 6)
        core = across(parts[1], 1)
        shape = (2, 8, 256, HEAD_DIM)
        kv_grad = finish(mine, parts[0].reshape(shape), core.reshape(shape), side.reshape(shape), cross.reshape(shape), kv, key_gain)
    with jax.named_scope("gains"):
        front, kv_grad = lax.optimization_barrier((front, kv_grad))
        rows = jnp.sum(front[:, 1024:1030].astype(jnp.float32).reshape(8, 2, 3, HEAD_DIM), axis=2)
        rows = over_four(rows, "seq", 1)
        other = across(rows, 4)
        rows = jnp.stack([jnp.where(half == 0, rows, other), jnp.where(half == 0, other, rows)], axis=1)
        rows = over_four(rows, "dp", 1).reshape(HEADS, 2, HEAD_DIM)
    with jax.named_scope("return"):
        got = across(front[:, 512:1024], 6)
        attended, query_grad = mover(unpack_front_kernel, "unpack_front", (ROWS, ROWS), mine, front, got)
        key_grad, value_grad = mover(unpack_kernel, "unpack", (ROWS, ROWS), along_z(kv_grad))
    return (attended[None], query_grad[None], key_grad[None], value_grad[None], rows[:, 0], rows[:, 1])


def solution(mesh):
    rows = P("dp", "seq", None)
    return jax.shard_map(
        body,
        mesh=mesh,
        in_specs=(rows, rows, rows, rows, P(), P(), P("dp", None, None, None), P("dp", None, None)),
        out_specs=(rows, rows, rows, rows, P(), P()),
        check_vma=False,
    )
```

```python
import functools
import math

import jax
import jax.numpy as jnp
from jax import lax
from jax.experimental import pallas as pl
from jax.experimental.pallas import tpu as pltpu
from jax.sharding import PartitionSpec as P

HEAD_DIM = 128
EPS = 1e-06
INV_ROOT = 1.0 / math.sqrt(HEAD_DIM)
LOG2E = math.log2(math.e)
NT = (((1,), (1,)), ((), ()))
TN = (((0,), (0,)), ((), ()))
NN = (((1,), (0,)), ((), ()))
GROUPS = 32
BUCKETS = (8, 6, 4, 2)
TOGETHER = 4
SEND_ORDER = (5, 3, 1, 7, 4, 2, 0, 6)


def dot(a, b, dims):
    return lax.dot_general(a, b, dims, preferred_element_type=jnp.float32)


def attend_kernel(info_ref, count_ref, list_ref, *refs):
    pieces = refs[:8]
    qg_hbm, query_gain_ref, key_gain_ref, og_hbm = refs[8:12]
    parts = refs[12:20]
    gain_query_ref, gain_key_ref, ktab, vtab, acc, qg_ref, og_ref, stage, order_ref, in_sems, out_sems = refs[20:]
    place_x_core = info_ref[0]
    head = info_ref[1]
    copies = [pltpu.make_async_copy(qg_hbm, qg_ref, in_sems.at[16])]
    for i, piece in enumerate(pieces):
        for j, table in enumerate((ktab, vtab)):
            copies.append(pltpu.make_async_copy(piece.at[j], table.at[pl.ds(i * 16, 16)], in_sems.at[2 * i + j]))
    for copy in copies:
        copy.start()

    def block_of(g):
        across = place_x_core ^ (6 * ((g >> 1) & 1))
        return (g >> 2) * 16 + across * 2 + (g & 1)

    stops = []
    stop = 0
    for which, most in enumerate(BUCKETS):
        below = BUCKETS[which + 1] if which + 1 < len(BUCKETS) else 0

        def place(g, at, most=most, below=below):
            count = count_ref[block_of(g)]
            inside = jnp.logical_and(count <= most, count > below)

            @pl.when(inside)
            def _():
                order_ref[at] = g

            return at + inside.astype(jnp.int32)

        stop = lax.fori_loop(0, GROUPS, place, jnp.int32(stop))
        stops.append(stop)

    @pl.loop(0, 128)
    def _(t):
        acc[t] = jnp.zeros((128, 256), jnp.float32)

    gain_query = query_gain_ref[pl.ds(head, 1), :]
    gain_key = key_gain_ref[pl.ds(head, 1), :]
    gain_query_ref[...] = jnp.zeros_like(gain_query_ref)
    gain_key_ref[...] = jnp.zeros_like(gain_key_ref)
    for copy in copies:
        copy.wait()

    zero = jnp.zeros((128, 128), jnp.bfloat16)

    def group(i, most, first):
        g = order_ref[i]
        block = block_of(g)
        live = count_ref[block]
        listed = [list_ref[block * 8 + j] for j in range(most)]
        spots = [(((c >> 1) & 7) ^ place_x_core) * 16 + (c >> 4) * 2 + (c & 1) for c in listed]
        row = pl.multiple_of(((g >> 1) & 1) * 512 + (g & 1) * 128, 128)
        wide = qg_ref[g >> 1, 0, g & 1].astype(jnp.float32)
        grad = qg_ref[g >> 1, 1, g & 1]
        scale = lax.rsqrt(jnp.mean(wide * wide, axis=-1, keepdims=True) + EPS)
        hat = wide * scale
        normed = (hat * gain_query).astype(jnp.bfloat16)
        keys = jnp.concatenate([ktab[t] for t in spots], axis=0)
        values = jnp.concatenate([vtab[t] for t in spots], axis=0)
        yield
        flat = dot(normed, keys, NT)
        scores = []
        for j in range(most):
            s = flat[:, j * 128:(j + 1) * 128]
            if j == most - 1 or (j and not first):
                s = jnp.where(j < live, s, -jnp.inf)
            scores.append(s)
        yield
        top = jnp.max(functools.reduce(jnp.maximum, scores), axis=-1, keepdims=True)
        yield
        exps = [jnp.exp2((s - top) * (INV_ROOT * LOG2E)) for s in scores]
        total = jnp.sum(functools.reduce(jnp.add, exps), axis=-1, keepdims=True)
        yield
        inverse = 1.0 / total
        weights = [(e * inverse).astype(jnp.bfloat16) for e in exps]
        attended = dot(jnp.concatenate(weights, axis=1), values, NN).astype(jnp.bfloat16)
        yield
        flat = dot(grad, values, NT)
        inner = jnp.sum(grad.astype(jnp.float32) * attended.astype(jnp.float32), axis=-1, keepdims=True)
        yield
        score_grads = []
        for j in range(most):
            wg = flat[:, j * 128:(j + 1) * 128]
            score_grads.append((weights[j].astype(jnp.float32) * (wg - inner)).astype(jnp.bfloat16))
        norm_grad = dot(jnp.concatenate(score_grads, axis=1), keys, NN) * INV_ROOT
        yield
        pair = jnp.concatenate(
            [jnp.concatenate([normed, zero], axis=1), jnp.concatenate([zero, grad], axis=1)], axis=0
        )
        terms = [dot(jnp.concatenate([score_grads[j], weights[j]], axis=0), pair, TN) for j in range(most)]
        weighted = norm_grad * gain_query
        mean = jnp.mean(weighted * wide, axis=-1, keepdims=True)
        query_grad = (scale * weighted - wide * (scale * scale * scale) * mean).astype(jnp.bfloat16)
        yield
        og_ref[g >> 2, pl.ds(row, 128)] = attended
        og_ref[g >> 2, pl.ds(row + 256, 128)] = query_grad
        for j in range(most):
            acc[spots[j]] += terms[j]
        gain_query_ref[0:1, :] += jnp.sum(norm_grad * hat, axis=0, keepdims=True)

    start = 0
    for which, most in enumerate(BUCKETS):
        stop = (stops[which] + TOGETHER - 1) // TOGETHER

        @pl.loop(start, stop)
        def _(step, most=most):
            running = [group(step * TOGETHER + u, most, u == 0) for u in range(TOGETHER)]
            while running:
                running = [one for one in running if next(one, running) is None]

        start = stop

    rows = pl.ds(0, 1024)
    back = [pltpu.make_async_copy(og_ref.at[:, rows], og_hbm.at[:, rows], out_sems.at[8])]
    back[0].start()
    for i in SEND_ORDER:

        @pl.loop(i * 16, i * 16 + 16, unroll=2)
        def _(t, i=i):
            both = acc[t]
            k = (both[:, :128] * INV_ROOT).astype(jnp.bfloat16)
            stage[i, 0, t - i * 16] = k
            stage[i, 1, t - i * 16] = both[:, 128:].astype(jnp.bfloat16)
            sums = jnp.sum(k.astype(jnp.float32) * ktab[t].astype(jnp.float32), axis=0, keepdims=True)
            gain_key_ref[0:1, :] += sums

        back.append(pltpu.make_async_copy(stage.at[i], parts[i], out_sems.at[i]))
        back[-1].start()
    split = []
    for wide in (gain_query_ref[0:1, :], gain_key_ref[0:1, :] / gain_key):
        for _ in range(3):
            split.append(wide.astype(jnp.bfloat16).astype(jnp.float32))
            wide = wide - split[-1]
    split = jnp.concatenate(split + [jnp.zeros((10, 128), jnp.float32)], axis=0).astype(jnp.bfloat16)
    for z in range(8):
        og_ref[z, 1024:1040] = split
    rows = pl.ds(1024, 16)
    back.append(pltpu.make_async_copy(og_ref.at[:, rows], og_hbm.at[:, rows], out_sems.at[9]))
    back[-1].start()
    for copy in back:
        copy.wait()


def attend(info, counts, lists, pieces, qg, query_gain, key_gain):
    smem = pl.BlockSpec(memory_space=pltpu.SMEM)
    vmem = pl.BlockSpec(memory_space=pltpu.VMEM)
    hbm = pl.BlockSpec(memory_space=pl.ANY)
    part = jax.ShapeDtypeStruct((2, 16, 128, 128), jnp.bfloat16)
    return pl.pallas_call(
        attend_kernel,
        out_shape=(jax.ShapeDtypeStruct((8, 1040, 128), jnp.bfloat16),) + (part,) * 8,
        in_specs=[smem] * 3 + [hbm] * 9 + [vmem] * 2,
        out_specs=(hbm,) * 9,
        scratch_shapes=[
            pltpu.VMEM((8, 128), jnp.float32),
            pltpu.VMEM((8, 128), jnp.float32),
            pltpu.VMEM((128, 128, 128), jnp.bfloat16),
            pltpu.VMEM((128, 128, 128), jnp.bfloat16),
            pltpu.VMEM((128, 128, 256), jnp.float32),
            pltpu.VMEM((16, 2, 2, 128, 128), jnp.bfloat16),
            pltpu.VMEM((8, 1040, 128), jnp.bfloat16),
            pltpu.VMEM((8, 2, 16, 128, 128), jnp.bfloat16),
            pltpu.SMEM((GROUPS,), jnp.int32),
            pltpu.SemaphoreType.DMA((17,)),
            pltpu.SemaphoreType.DMA((10,)),
        ],
        compiler_params=pltpu.CompilerParams(vmem_limit_bytes=56 * 1024 * 1024),
        cost_estimate=pl.CostEstimate(flops=6 * 10**9, bytes_accessed=20 * 2**20, transcendentals=4 * 2**20),
        name="attend",
    )(info, counts, lists, *pieces, qg, query_gain, key_gain)


HEADS = 16
ALONG_Z = [[8 * z + rest for z in range(8)] for rest in range(8)]
ROWS = jax.ShapeDtypeStruct((256, HEADS * HEAD_DIM), jnp.bfloat16)
PAIRS = jax.ShapeDtypeStruct((8, 2, 2, 256, HEAD_DIM), jnp.bfloat16)
HALF_PAIRS = jax.ShapeDtypeStruct((8, 2, 256, HEAD_DIM), jnp.bfloat16)


def columns(head):
    if isinstance(head, int):
        return pl.ds(head * HEAD_DIM, HEAD_DIM)
    return pl.ds(pl.multiple_of(head * HEAD_DIM, HEAD_DIM), HEAD_DIM)


def staged(groups, in_sems, out_sems):
    loads, stores = [], []
    for ins, _ in groups:
        made = [pltpu.make_async_copy(a, b, in_sems.at[sum(map(len, loads)) + i]) for i, (a, b) in enumerate(ins)]
        loads.append(made)
    for made in loads:
        for copy in made:
            copy.start()
    for made, (_, outs) in zip(loads, groups):
        for copy in made:
            copy.wait()
        for a, b in outs:
            stores.append(pltpu.make_async_copy(a, b, out_sems.at[len(stores)]))
            stores[-1].start()
    for copy in stores:
        copy.wait()


def pack_kernel(a_ref, b_ref, out_ref, buf, in_sems, out_sems):
    staged([([(ref.at[:, columns(2 * z + hh)], buf.at[z, hh, i])
              for hh in range(2) for i, ref in enumerate((a_ref, b_ref))], [(buf.at[z], out_ref.at[z])])
            for z in range(8)], in_sems, out_sems)


def give_kernel(mine_ref, a_ref, b_ref, out_ref, buf, in_sems, out_sems):
    staged([([(ref.at[:, columns(2 * z + 1 - mine_ref[0])], buf.at[z, i]) for i, ref in enumerate((a_ref, b_ref))],
             [(buf.at[z], out_ref.at[z])]) for z in range(8)], in_sems, out_sems)


def pack_pair_kernel(mine_ref, a_ref, b_ref, got_ref, out_ref, buf, in_sems, out_sems):
    staged([([(got_ref.at[z], buf.at[z, 1])]
             + [(ref.at[:, columns(2 * z + mine_ref[0])], buf.at[z, 0, i]) for i, ref in enumerate((a_ref, b_ref))],
             [(buf.at[z], out_ref.at[z])]) for z in range(8)], in_sems, out_sems)


def plane_columns(z):
    return pl.ds(z * 2 * HEAD_DIM, 2 * HEAD_DIM)


def unpack_kernel(in_ref, a_ref, b_ref, buf, in_sems, out_sems):
    staged([([(in_ref.at[z, hh, i], buf.at[i, :, columns(2 * z + hh)]) for hh in range(2) for i in range(2)],
             [(buf.at[i, :, plane_columns(z)], ref.at[:, plane_columns(z)]) for i, ref in enumerate((a_ref, b_ref))])
            for z in range(8)], in_sems, out_sems)


def unpack_front_kernel(mine_ref, in_ref, got_ref, a_ref, b_ref, buf, in_sems, out_sems):
    half = mine_ref[0]
    staged([([(in_ref.at[z, pl.ds(i * 256, 256)], buf.at[i, :, columns(2 * z + half)]) for i in range(2)]
             + [(got_ref.at[z, pl.ds(i * 256, 256)], buf.at[i, :, columns(2 * z + 1 - half)]) for i in range(2)],
             [(buf.at[i, :, plane_columns(z)], ref.at[:, plane_columns(z)]) for i, ref in enumerate((a_ref, b_ref))])
            for z in range(8)], in_sems, out_sems)


def mover(kernel, name, out_shape, *args):
    smem = pl.BlockSpec(memory_space=pltpu.SMEM)
    hbm = pl.BlockSpec(memory_space=pl.ANY)
    many = isinstance(out_shape, tuple)
    return pl.pallas_call(
        kernel,
        out_shape=out_shape,
        in_specs=[smem if a.dtype == jnp.int32 else hbm for a in args],
        out_specs=(hbm,) * len(out_shape) if many else hbm,
        scratch_shapes=[
            pltpu.VMEM((2,) + ROWS.shape if many else out_shape.shape, jnp.bfloat16),
            pltpu.SemaphoreType.DMA((32,)),
            pltpu.SemaphoreType.DMA((16,)),
        ],
        compiler_params=pltpu.CompilerParams(vmem_limit_bytes=56 * 1024 * 1024),
        cost_estimate=pl.CostEstimate(flops=0, bytes_accessed=2**22, transcendentals=0),
        name=name,
    )(*args)


def norm_kernel(mine_ref, kv_hbm, gain_ref, own_hbm, cross_hbm, kv, out, in_sems, out_sems):
    half = mine_ref[0]
    plane = mine_ref[1]
    loads = [pltpu.make_async_copy(kv_hbm.at[z], kv.at[z], in_sems.at[z]) for z in range(8)]
    for load in loads:
        load.start()
    stores = []
    for z in range(8):
        loads[z].wait()
        for which, target in ((0, cross_hbm), (1, own_hbm)):
            hh = half if which else 1 - half
            wide = kv[z, hh, 0].astype(jnp.float32)
            scale = lax.rsqrt(jnp.mean(wide * wide, axis=-1, keepdims=True) + EPS)
            out[which, z] = (wide * scale * gain_ref[pl.ds(2 * plane + hh, 1), :]).astype(jnp.bfloat16)
            stores.append(pltpu.make_async_copy(out.at[which, z], target.at[0, z], out_sems.at[4 * z + 2 * which]))
            stores.append(pltpu.make_async_copy(kv.at[z, hh, 1], target.at[1, z], out_sems.at[4 * z + 2 * which + 1]))
            stores[-2].start()
            stores[-1].start()
    for store in stores:
        store.wait()


def norm(mine, kv, gain):
    hbm = pl.BlockSpec(memory_space=pl.ANY)
    piece = jax.ShapeDtypeStruct((2, 8, 256, HEAD_DIM), jnp.bfloat16)
    return pl.pallas_call(
        norm_kernel,
        out_shape=(piece, piece),
        in_specs=[pl.BlockSpec(memory_space=pltpu.SMEM), hbm, pl.BlockSpec(memory_space=pltpu.VMEM)],
        out_specs=(hbm, hbm),
        scratch_shapes=[
            pltpu.VMEM((8, 2, 2, 256, HEAD_DIM), jnp.bfloat16),
            pltpu.VMEM((2, 8, 256, HEAD_DIM), jnp.bfloat16),
            pltpu.SemaphoreType.DMA((8,)),
            pltpu.SemaphoreType.DMA((32,)),
        ],
        compiler_params=pltpu.CompilerParams(vmem_limit_bytes=56 * 1024 * 1024),
        cost_estimate=pl.CostEstimate(flops=10**7, bytes_accessed=2**22, transcendentals=2**13),
        name="norm",
    )(mine, kv, gain)


def finish_kernel(mine_ref, part_hbm, core_hbm, side_hbm, far_hbm, kv_hbm, gain_ref, out_hbm,
                  sums, kv, out, in_sems, out_sems):
    half = mine_ref[0]
    plane = mine_ref[1]
    loads = []
    for z in range(8):
        for i, ref in enumerate((part_hbm, core_hbm, side_hbm, far_hbm)):
            loads.append(pltpu.make_async_copy(ref.at[:, z], sums.at[i, :, z], in_sems.at[5 * z + i]))
        loads.append(pltpu.make_async_copy(kv_hbm.at[z, :, 0], kv.at[z], in_sems.at[5 * z + 4]))
    for load in loads:
        load.start()
    stores = []
    for z in range(8):
        for load in loads[5 * z:5 * z + 5]:
            load.wait()
        for own in (True, False):
            hh = half if own else 1 - half
            gain = gain_ref[pl.ds(2 * plane + hh, 1), :]
            if own:
                total = [functools.reduce(jnp.add, [sums[j, i, z].astype(jnp.float32) for j in range(3)]) for i in range(2)]
            else:
                total = [sums[3, i, z].astype(jnp.float32) for i in range(2)]
            wide = kv[z, hh].astype(jnp.float32)
            scale = lax.rsqrt(jnp.mean(wide * wide, axis=-1, keepdims=True) + EPS)
            weighted = total[0] * gain
            inner = jnp.mean(weighted * wide, axis=-1, keepdims=True)
            out[z, hh, 0] = (scale * weighted - wide * (scale * scale * scale) * inner).astype(jnp.bfloat16)
            out[z, hh, 1] = total[1].astype(jnp.bfloat16)
        stores.append(pltpu.make_async_copy(out.at[z], out_hbm.at[z], out_sems.at[z]))
        stores[-1].start()
    for store in stores:
        store.wait()


def finish(mine, part, core, side, far, kv, gain):
    hbm = pl.BlockSpec(memory_space=pl.ANY)
    return pl.pallas_call(
        finish_kernel,
        out_shape=PAIRS,
        in_specs=[pl.BlockSpec(memory_space=pltpu.SMEM)] + [hbm] * 5 + [pl.BlockSpec(memory_space=pltpu.VMEM)],
        out_specs=hbm,
        scratch_shapes=[
            pltpu.VMEM((4, 2, 8, 256, HEAD_DIM), jnp.bfloat16),
            pltpu.VMEM((8, 2, 256, HEAD_DIM), jnp.bfloat16),
            pltpu.VMEM((8, 2, 2, 256, HEAD_DIM), jnp.bfloat16),
            pltpu.SemaphoreType.DMA((40,)),
            pltpu.SemaphoreType.DMA((8,)),
        ],
        compiler_params=pltpu.CompilerParams(vmem_limit_bytes=56 * 1024 * 1024),
        cost_estimate=pl.CostEstimate(flops=10**7, bytes_accessed=2**23, transcendentals=2**13),
        name="finish",
    )(mine, part, core, side, far, kv, gain)


def along_z(array):
    return lax.all_to_all(array, "seq", split_axis=0, concat_axis=0, axis_index_groups=ALONG_Z, tiled=True)


def across(array, flip):
    return lax.ppermute(array, "seq", [(i, i ^ flip) for i in range(64)])


def wide_sum(*arrays):
    return functools.reduce(jnp.add, [a.astype(jnp.float32) for a in arrays]).astype(jnp.bfloat16)


def over_four(array, axis, step):
    size = lax.axis_size(axis)
    one, two, three = [lax.ppermute(array, axis, [(i, i ^ (step * f)) for i in range(size)]) for f in (1, 2, 3)]
    return (array + one) + (two + three)


def body(query_rows, key_rows, value_rows, output_grad, query_gain, key_gain, block_list, block_count):
    position = lax.axis_index("seq")
    head = position // 4
    plane = position // 8
    half = head % 2
    lists = lax.dynamic_slice_in_dim(block_list[0], head, 1, 0).reshape(1024)
    counts = lax.dynamic_slice_in_dim(block_count[0], head, 1, 0).reshape(128)
    info = jnp.stack([position % 8, head]).astype(jnp.int32)
    mine = jnp.stack([half, plane]).astype(jnp.int32)

    with jax.named_scope("gather"):
        kv = along_z(mover(pack_kernel, "pack", PAIRS, key_rows[0], value_rows[0]))
        got = across(mover(give_kernel, "give", HALF_PAIRS, mine, query_rows[0], output_grad[0]), 6)
        pair_send = mover(pack_pair_kernel, "pack_pair", PAIRS, mine, query_rows[0], output_grad[0], got)
        pair_send, kv, lists, counts, info = lax.optimization_barrier((pair_send, kv, lists, counts, info))
        own, cross_send = norm(mine, kv, key_gain)
        cross = across(cross_send, 6)
        side = across(own, 2)
        query_pair = along_z(pair_send)
        far = across(cross, 2)
        pieces = []
        for piece in (own, side, far, cross):
            pieces += [piece, across(piece, 1)]
        pieces = [p.reshape(2, 16, 128, 128) for p in pieces]
    with jax.named_scope("attend"):
        outs = attend(info, counts, lists, pieces, query_pair.reshape(16, 2, 2, 128, 128), query_gain, key_gain)
    front, parts = outs[0], outs[1:9]
    with jax.named_scope("return"):
        far = wide_sum(parts[4], across(parts[5], 1))
        side = wide_sum(parts[2], across(parts[3], 1))
        far = across(far, 2)
        front, side = lax.optimization_barrier((front, side))
        front = along_z(front)
        far, side = lax.optimization_barrier((far, side))
        side = across(side, 2)
        cross = across(wide_sum(parts[6], across(parts[7], 1), far), 6)
        core = across(parts[1], 1)
        shape = (2, 8, 256, HEAD_DIM)
        kv_grad = finish(mine, parts[0].reshape(shape), core.reshape(shape), side.reshape(shape), cross.reshape(shape), kv, key_gain)
    with jax.named_scope("gains"):
        front, kv_grad = lax.optimization_barrier((front, kv_grad))
        rows = jnp.sum(front[:, 1024:1030].astype(jnp.float32).reshape(8, 2, 3, HEAD_DIM), axis=2)
        rows = over_four(rows, "seq", 1)
        other = across(rows, 4)
        rows = jnp.stack([jnp.where(half == 0, rows, other), jnp.where(half == 0, other, rows)], axis=1)
        rows = over_four(rows, "dp", 1).reshape(HEADS, 2, HEAD_DIM)
    with jax.named_scope("return"):
        got = across(front[:, 512:1024], 6)
        attended, query_grad = mover(unpack_front_kernel, "unpack_front", (ROWS, ROWS), mine, front, got)
        key_grad, value_grad = mover(unpack_kernel, "unpack", (ROWS, ROWS), along_z(kv_grad))
    return (attended[None], query_grad[None], key_grad[None], value_grad[None], rows[:, 0], rows[:, 1])


def solution(mesh):
    rows = P("dp", "seq", None)
    return jax.shard_map(
        body,
        mesh=mesh,
        in_specs=(rows, rows, rows, rows, P(), P(), P("dp", None, None, None), P("dp", None, None)),
        out_specs=(rows, rows, rows, rows, P(), P()),
        check_vma=False,
    )
```

```python
import functools
import math

import jax
import jax.numpy as jnp
from jax import lax
from jax.experimental import pallas as pl
from jax.experimental.pallas import tpu as pltpu
from jax.sharding import PartitionSpec as P

HEAD_DIM = 128
EPS = 1e-06
INV_ROOT = 1.0 / math.sqrt(HEAD_DIM)
LOG2E = math.log2(math.e)
NT = (((1,), (1,)), ((), ()))
TN = (((0,), (0,)), ((), ()))
NN = (((1,), (0,)), ((), ()))
GROUPS = 32
BUCKETS = (8, 6, 4, 2)
TOGETHER = 4
SEND_ORDER = (5, 3, 1, 7, 4, 2, 0, 6)


def dot(a, b, dims):
    return lax.dot_general(a, b, dims, preferred_element_type=jnp.float32)


def attend_kernel(info_ref, count_ref, list_ref, *refs):
    pieces = refs[:8]
    qg_hbm, query_gain_ref, key_gain_ref, og_hbm = refs[8:12]
    parts = refs[12:20]
    gain_query_ref, gain_key_ref, ktab, vtab, acc, qg_ref, og_ref, stage, order_ref, in_sems, out_sems = refs[20:]
    place_x_core = info_ref[0]
    head = info_ref[1]
    copies = [pltpu.make_async_copy(qg_hbm, qg_ref, in_sems.at[16])]
    for i, piece in enumerate(pieces):
        for j, table in enumerate((ktab, vtab)):
            copies.append(pltpu.make_async_copy(piece.at[j], table.at[pl.ds(i * 16, 16)], in_sems.at[2 * i + j]))
    for copy in copies:
        copy.start()

    def block_of(g):
        across = place_x_core ^ (6 * ((g >> 1) & 1))
        return (g >> 2) * 16 + across * 2 + (g & 1)

    stops = []
    stop = 0
    for which, most in enumerate(BUCKETS):
        below = BUCKETS[which + 1] if which + 1 < len(BUCKETS) else 0

        def place(g, at, most=most, below=below):
            count = count_ref[block_of(g)]
            inside = jnp.logical_and(count <= most, count > below)

            @pl.when(inside)
            def _():
                order_ref[at] = g

            return at + inside.astype(jnp.int32)

        stop = lax.fori_loop(0, GROUPS, place, jnp.int32(stop))
        stops.append(stop)

    @pl.loop(0, 128)
    def _(t):
        acc[t] = jnp.zeros((128, 256), jnp.float32)

    gain_query = query_gain_ref[pl.ds(head, 1), :]
    gain_key = key_gain_ref[pl.ds(head, 1), :]
    gain_query_ref[...] = jnp.zeros_like(gain_query_ref)
    gain_key_ref[...] = jnp.zeros_like(gain_key_ref)
    for copy in copies:
        copy.wait()

    zero = jnp.zeros((128, 128), jnp.bfloat16)

    def group(i, most, first):
        g = order_ref[i]
        block = block_of(g)
        live = count_ref[block]
        listed = [list_ref[block * 8 + j] for j in range(most)]
        spots = [(((c >> 1) & 7) ^ place_x_core) * 16 + (c >> 4) * 2 + (c & 1) for c in listed]
        row = pl.multiple_of(((g >> 1) & 1) * 512 + (g & 1) * 128, 128)
        wide = qg_ref[g >> 1, 0, g & 1].astype(jnp.float32)
        grad = qg_ref[g >> 1, 1, g & 1]
        scale = lax.rsqrt(jnp.mean(wide * wide, axis=-1, keepdims=True) + EPS)
        hat = wide * scale
        normed = (hat * gain_query).astype(jnp.bfloat16)
        keys = jnp.concatenate([ktab[t] for t in spots], axis=0)
        values = jnp.concatenate([vtab[t] for t in spots], axis=0)
        yield
        flat = dot(normed, keys, NT)
        scores = []
        for j in range(most):
            s = flat[:, j * 128:(j + 1) * 128]
            if j == most - 1 or (j and not first):
                s = jnp.where(j < live, s, -jnp.inf)
            scores.append(s)
        yield
        top = jnp.max(functools.reduce(jnp.maximum, scores), axis=-1, keepdims=True)
        yield
        exps = [jnp.exp2((s - top) * (INV_ROOT * LOG2E)) for s in scores]
        total = jnp.sum(functools.reduce(jnp.add, exps), axis=-1, keepdims=True)
        yield
        inverse = 1.0 / total
        weights = [(e * inverse).astype(jnp.bfloat16) for e in exps]
        attended = dot(jnp.concatenate(weights, axis=1), values, NN).astype(jnp.bfloat16)
        yield
        flat = dot(grad, values, NT)
        inner = jnp.sum(grad.astype(jnp.float32) * attended.astype(jnp.float32), axis=-1, keepdims=True)
        yield
        score_grads = []
        for j in range(most):
            wg = flat[:, j * 128:(j + 1) * 128]
            score_grads.append((weights[j].astype(jnp.float32) * (wg - inner)).astype(jnp.bfloat16))
        norm_grad = dot(jnp.concatenate(score_grads, axis=1), keys, NN) * INV_ROOT
        yield
        pair = jnp.concatenate(
            [jnp.concatenate([normed, zero], axis=1), jnp.concatenate([zero, grad], axis=1)], axis=0
        )
        terms = [dot(jnp.concatenate([score_grads[j], weights[j]], axis=0), pair, TN) for j in range(most)]
        weighted = norm_grad * gain_query
        mean = jnp.mean(weighted * wide, axis=-1, keepdims=True)
        query_grad = (scale * weighted - wide * (scale * scale * scale) * mean).astype(jnp.bfloat16)
        yield
        og_ref[g >> 2, pl.ds(row, 128)] = attended
        og_ref[g >> 2, pl.ds(row + 256, 128)] = query_grad
        for j in range(most):
            acc[spots[j]] += terms[j]
        gain_query_ref[0:1, :] += jnp.sum(norm_grad * hat, axis=0, keepdims=True)

    start = 0
    for which, most in enumerate(BUCKETS):
        stop = (stops[which] + TOGETHER - 1) // TOGETHER

        @pl.loop(start, stop)
        def _(step, most=most):
            running = [group(step * TOGETHER + u, most, u == 0) for u in range(TOGETHER)]
            while running:
                running = [one for one in running if next(one, running) is None]

        start = stop

    rows = pl.ds(0, 1024)
    back = [pltpu.make_async_copy(og_ref.at[:, rows], og_hbm.at[:, rows], out_sems.at[8])]
    back[0].start()
    for i in SEND_ORDER:

        @pl.loop(i * 16, i * 16 + 16, unroll=2)
        def _(t, i=i):
            both = acc[t]
            k = (both[:, :128] * INV_ROOT).astype(jnp.bfloat16)
            stage[i, 0, t - i * 16] = k
            stage[i, 1, t - i * 16] = both[:, 128:].astype(jnp.bfloat16)
            sums = jnp.sum(k.astype(jnp.float32) * ktab[t].astype(jnp.float32), axis=0, keepdims=True)
            gain_key_ref[0:1, :] += sums

        back.append(pltpu.make_async_copy(stage.at[i], parts[i], out_sems.at[i]))
        back[-1].start()
    split = []
    for wide in (gain_query_ref[0:1, :], gain_key_ref[0:1, :] / gain_key):
        for _ in range(3):
            split.append(wide.astype(jnp.bfloat16).astype(jnp.float32))
            wide = wide - split[-1]
    split = jnp.concatenate(split + [jnp.zeros((10, 128), jnp.float32)], axis=0).astype(jnp.bfloat16)
    for z in range(8):
        og_ref[z, 1024:1040] = split
    rows = pl.ds(1024, 16)
    back.append(pltpu.make_async_copy(og_ref.at[:, rows], og_hbm.at[:, rows], out_sems.at[9]))
    back[-1].start()
    for copy in back:
        copy.wait()


def attend(info, counts, lists, pieces, qg, query_gain, key_gain):
    smem = pl.BlockSpec(memory_space=pltpu.SMEM)
    vmem = pl.BlockSpec(memory_space=pltpu.VMEM)
    hbm = pl.BlockSpec(memory_space=pl.ANY)
    part = jax.ShapeDtypeStruct((2, 16, 128, 128), jnp.bfloat16)
    return pl.pallas_call(
        attend_kernel,
        out_shape=(jax.ShapeDtypeStruct((8, 1040, 128), jnp.bfloat16),) + (part,) * 8,
        in_specs=[smem] * 3 + [hbm] * 9 + [vmem] * 2,
        out_specs=(hbm,) * 9,
        scratch_shapes=[
            pltpu.VMEM((8, 128), jnp.float32),
            pltpu.VMEM((8, 128), jnp.float32),
            pltpu.VMEM((128, 128, 128), jnp.bfloat16),
            pltpu.VMEM((128, 128, 128), jnp.bfloat16),
            pltpu.VMEM((128, 128, 256), jnp.float32),
            pltpu.VMEM((16, 2, 2, 128, 128), jnp.bfloat16),
            pltpu.VMEM((8, 1040, 128), jnp.bfloat16),
            pltpu.VMEM((8, 2, 16, 128, 128), jnp.bfloat16),
            pltpu.SMEM((GROUPS,), jnp.int32),
            pltpu.SemaphoreType.DMA((17,)),
            pltpu.SemaphoreType.DMA((10,)),
        ],
        compiler_params=pltpu.CompilerParams(vmem_limit_bytes=56 * 1024 * 1024),
        cost_estimate=pl.CostEstimate(flops=6 * 10**9, bytes_accessed=20 * 2**20, transcendentals=4 * 2**20),
        name="attend",
    )(info, counts, lists, *pieces, qg, query_gain, key_gain)


HEADS = 16
ALONG_Z = [[8 * z + rest for z in range(8)] for rest in range(8)]
ROWS = jax.ShapeDtypeStruct((256, HEADS * HEAD_DIM), jnp.bfloat16)
PAIRS = jax.ShapeDtypeStruct((8, 2, 2, 256, HEAD_DIM), jnp.bfloat16)
HALF_PAIRS = jax.ShapeDtypeStruct((8, 2, 256, HEAD_DIM), jnp.bfloat16)


def columns(head):
    if isinstance(head, int):
        return pl.ds(head * HEAD_DIM, HEAD_DIM)
    return pl.ds(pl.multiple_of(head * HEAD_DIM, HEAD_DIM), HEAD_DIM)


def staged(groups, in_sems, out_sems):
    loads, stores = [], []
    for ins, _ in groups:
        made = [pltpu.make_async_copy(a, b, in_sems.at[sum(map(len, loads)) + i]) for i, (a, b) in enumerate(ins)]
        loads.append(made)
    for made in loads:
        for copy in made:
            copy.start()
    for made, (_, outs) in zip(loads, groups):
        for copy in made:
            copy.wait()
        for a, b in outs:
            stores.append(pltpu.make_async_copy(a, b, out_sems.at[len(stores)]))
            stores[-1].start()
    for copy in stores:
        copy.wait()


def pack_kernel(a_ref, b_ref, out_ref, buf, in_sems, out_sems):
    staged([([(ref.at[:, columns(2 * z + hh)], buf.at[z, hh, i])
              for hh in range(2) for i, ref in enumerate((a_ref, b_ref))], [(buf.at[z], out_ref.at[z])])
            for z in range(8)], in_sems, out_sems)


def give_kernel(mine_ref, a_ref, b_ref, out_ref, buf, in_sems, out_sems):
    staged([([(ref.at[:, columns(2 * z + 1 - mine_ref[0])], buf.at[z, i]) for i, ref in enumerate((a_ref, b_ref))],
             [(buf.at[z], out_ref.at[z])]) for z in range(8)], in_sems, out_sems)


def pack_pair_kernel(mine_ref, a_ref, b_ref, got_ref, out_ref, buf, in_sems, out_sems):
    staged([([(got_ref.at[z], buf.at[z, 1])]
             + [(ref.at[:, columns(2 * z + mine_ref[0])], buf.at[z, 0, i]) for i, ref in enumerate((a_ref, b_ref))],
             [(buf.at[z], out_ref.at[z])]) for z in range(8)], in_sems, out_sems)


def plane_columns(z):
    return pl.ds(z * 2 * HEAD_DIM, 2 * HEAD_DIM)


def unpack_kernel(in_ref, a_ref, b_ref, buf, in_sems, out_sems):
    staged([([(in_ref.at[z, hh, i], buf.at[i, :, columns(2 * z + hh)]) for hh in range(2) for i in range(2)],
             [(buf.at[i, :, plane_columns(z)], ref.at[:, plane_columns(z)]) for i, ref in enumerate((a_ref, b_ref))])
            for z in range(8)], in_sems, out_sems)


def unpack_front_kernel(mine_ref, in_ref, got_ref, a_ref, b_ref, buf, in_sems, out_sems):
    half = mine_ref[0]
    staged([([(in_ref.at[z, pl.ds(i * 256, 256)], buf.at[i, :, columns(2 * z + half)]) for i in range(2)]
             + [(got_ref.at[z, pl.ds(i * 256, 256)], buf.at[i, :, columns(2 * z + 1 - half)]) for i in range(2)],
             [(buf.at[i, :, plane_columns(z)], ref.at[:, plane_columns(z)]) for i, ref in enumerate((a_ref, b_ref))])
            for z in range(8)], in_sems, out_sems)


def mover(kernel, name, out_shape, *args):
    smem = pl.BlockSpec(memory_space=pltpu.SMEM)
    hbm = pl.BlockSpec(memory_space=pl.ANY)
    many = isinstance(out_shape, tuple)
    return pl.pallas_call(
        kernel,
        out_shape=out_shape,
        in_specs=[smem if a.dtype == jnp.int32 else hbm for a in args],
        out_specs=(hbm,) * len(out_shape) if many else hbm,
        scratch_shapes=[
            pltpu.VMEM((2,) + ROWS.shape if many else out_shape.shape, jnp.bfloat16),
            pltpu.SemaphoreType.DMA((32,)),
            pltpu.SemaphoreType.DMA((16,)),
        ],
        compiler_params=pltpu.CompilerParams(vmem_limit_bytes=56 * 1024 * 1024),
        cost_estimate=pl.CostEstimate(flops=0, bytes_accessed=2**22, transcendentals=0),
        name=name,
    )(*args)


def norm_kernel(mine_ref, kv_hbm, gain_ref, own_hbm, cross_hbm, kv, out, in_sems, out_sems):
    half = mine_ref[0]
    plane = mine_ref[1]
    loads = [pltpu.make_async_copy(kv_hbm.at[z], kv.at[z], in_sems.at[z]) for z in range(8)]
    for load in loads:
        load.start()
    stores = []
    for z in range(8):
        loads[z].wait()
        for which, target in ((0, cross_hbm), (1, own_hbm)):
            hh = half if which else 1 - half
            wide = kv[z, hh, 0].astype(jnp.float32)
            scale = lax.rsqrt(jnp.mean(wide * wide, axis=-1, keepdims=True) + EPS)
            out[which, z] = (wide * scale * gain_ref[pl.ds(2 * plane + hh, 1), :]).astype(jnp.bfloat16)
            stores.append(pltpu.make_async_copy(out.at[which, z], target.at[0, z], out_sems.at[4 * z + 2 * which]))
            stores.append(pltpu.make_async_copy(kv.at[z, hh, 1], target.at[1, z], out_sems.at[4 * z + 2 * which + 1]))
            stores[-2].start()
            stores[-1].start()
    for store in stores:
        store.wait()


def norm(mine, kv, gain):
    hbm = pl.BlockSpec(memory_space=pl.ANY)
    piece = jax.ShapeDtypeStruct((2, 8, 256, HEAD_DIM), jnp.bfloat16)
    return pl.pallas_call(
        norm_kernel,
        out_shape=(piece, piece),
        in_specs=[pl.BlockSpec(memory_space=pltpu.SMEM), hbm, pl.BlockSpec(memory_space=pltpu.VMEM)],
        out_specs=(hbm, hbm),
        scratch_shapes=[
            pltpu.VMEM((8, 2, 2, 256, HEAD_DIM), jnp.bfloat16),
            pltpu.VMEM((2, 8, 256, HEAD_DIM), jnp.bfloat16),
            pltpu.SemaphoreType.DMA((8,)),
            pltpu.SemaphoreType.DMA((32,)),
        ],
        compiler_params=pltpu.CompilerParams(vmem_limit_bytes=56 * 1024 * 1024),
        cost_estimate=pl.CostEstimate(flops=10**7, bytes_accessed=2**22, transcendentals=2**13),
        name="norm",
    )(mine, kv, gain)


def finish_kernel(mine_ref, part_hbm, core_hbm, side_hbm, far_hbm, kv_hbm, gain_ref, out_hbm,
                  sums, kv, out, in_sems, out_sems):
    half = mine_ref[0]
    plane = mine_ref[1]
    loads = []
    for z in range(8):
        for i, ref in enumerate((part_hbm, core_hbm, side_hbm, far_hbm)):
            loads.append(pltpu.make_async_copy(ref.at[:, z], sums.at[i, :, z], in_sems.at[5 * z + i]))
        loads.append(pltpu.make_async_copy(kv_hbm.at[z, :, 0], kv.at[z], in_sems.at[5 * z + 4]))
    for load in loads:
        load.start()
    stores = []
    for z in range(8):
        for load in loads[5 * z:5 * z + 5]:
            load.wait()
        for own in (True, False):
            hh = half if own else 1 - half
            gain = gain_ref[pl.ds(2 * plane + hh, 1), :]
            if own:
                total = [functools.reduce(jnp.add, [sums[j, i, z].astype(jnp.float32) for j in range(3)]) for i in range(2)]
            else:
                total = [sums[3, i, z].astype(jnp.float32) for i in range(2)]
            wide = kv[z, hh].astype(jnp.float32)
            scale = lax.rsqrt(jnp.mean(wide * wide, axis=-1, keepdims=True) + EPS)
            weighted = total[0] * gain
            inner = jnp.mean(weighted * wide, axis=-1, keepdims=True)
            out[z, hh, 0] = (scale * weighted - wide * (scale * scale * scale) * inner).astype(jnp.bfloat16)
            out[z, hh, 1] = total[1].astype(jnp.bfloat16)
        stores.append(pltpu.make_async_copy(out.at[z], out_hbm.at[z], out_sems.at[z]))
        stores[-1].start()
    for store in stores:
        store.wait()


def finish(mine, part, core, side, far, kv, gain):
    hbm = pl.BlockSpec(memory_space=pl.ANY)
    return pl.pallas_call(
        finish_kernel,
        out_shape=PAIRS,
        in_specs=[pl.BlockSpec(memory_space=pltpu.SMEM)] + [hbm] * 5 + [pl.BlockSpec(memory_space=pltpu.VMEM)],
        out_specs=hbm,
        scratch_shapes=[
            pltpu.VMEM((4, 2, 8, 256, HEAD_DIM), jnp.bfloat16),
            pltpu.VMEM((8, 2, 256, HEAD_DIM), jnp.bfloat16),
            pltpu.VMEM((8, 2, 2, 256, HEAD_DIM), jnp.bfloat16),
            pltpu.SemaphoreType.DMA((40,)),
            pltpu.SemaphoreType.DMA((8,)),
        ],
        compiler_params=pltpu.CompilerParams(vmem_limit_bytes=56 * 1024 * 1024),
        cost_estimate=pl.CostEstimate(flops=10**7, bytes_accessed=2**23, transcendentals=2**13),
        name="finish",
    )(mine, part, core, side, far, kv, gain)


def along_z(array):
    return lax.all_to_all(array, "seq", split_axis=0, concat_axis=0, axis_index_groups=ALONG_Z, tiled=True)


def across(array, flip):
    return lax.ppermute(array, "seq", [(i, i ^ flip) for i in range(64)])


def wide_sum(*arrays):
    return functools.reduce(jnp.add, [a.astype(jnp.float32) for a in arrays]).astype(jnp.bfloat16)


def over_four(array, axis, step):
    size = lax.axis_size(axis)
    one, two, three = [lax.ppermute(array, axis, [(i, i ^ (step * f)) for i in range(size)]) for f in (1, 2, 3)]
    return (array + one) + (two + three)


def body(query_rows, key_rows, value_rows, output_grad, query_gain, key_gain, block_list, block_count):
    position = lax.axis_index("seq")
    head = position // 4
    plane = position // 8
    half = head % 2
    lists = lax.dynamic_slice_in_dim(block_list[0], head, 1, 0).reshape(1024)
    counts = lax.dynamic_slice_in_dim(block_count[0], head, 1, 0).reshape(128)
    info = jnp.stack([position % 8, head]).astype(jnp.int32)
    mine = jnp.stack([half, plane]).astype(jnp.int32)

    with jax.named_scope("gather"):
        kv = along_z(mover(pack_kernel, "pack", PAIRS, key_rows[0], value_rows[0]))
        got = across(mover(give_kernel, "give", HALF_PAIRS, mine, query_rows[0], output_grad[0]), 6)
        pair_send = mover(pack_pair_kernel, "pack_pair", PAIRS, mine, query_rows[0], output_grad[0], got)
        pair_send, kv, lists, counts, info = lax.optimization_barrier((pair_send, kv, lists, counts, info))
        own, cross_send = norm(mine, kv, key_gain)
        cross = across(cross_send, 6)
        side = across(own, 2)
        query_pair = along_z(pair_send)
        far = across(cross, 2)
        pieces = []
        for piece in (own, side, far, cross):
            pieces += [piece, across(piece, 1)]
        pieces = [p.reshape(2, 16, 128, 128) for p in pieces]
    with jax.named_scope("attend"):
        outs = attend(info, counts, lists, pieces, query_pair.reshape(16, 2, 2, 128, 128), query_gain, key_gain)
    front, parts = outs[0], outs[1:9]
    with jax.named_scope("return"):
        far = wide_sum(parts[4], across(parts[5], 1))
        far, side = lax.optimization_barrier((far, across(parts[3], 1)))
        side = wide_sum(parts[2], side)
        far = across(far, 2)
        front, side = lax.optimization_barrier((front, side))
        front = along_z(front)
        far, side = lax.optimization_barrier((far, side))
        side = across(side, 2)
        cross = across(wide_sum(parts[6], across(parts[7], 1), far), 6)
        core = across(parts[1], 1)
        shape = (2, 8, 256, HEAD_DIM)
        kv_grad = finish(mine, parts[0].reshape(shape), core.reshape(shape), side.reshape(shape), cross.reshape(shape), kv, key_gain)
    with jax.named_scope("gains"):
        front, kv_grad = lax.optimization_barrier((front, kv_grad))
        rows = jnp.sum(front[:, 1024:1030].astype(jnp.float32).reshape(8, 2, 3, HEAD_DIM), axis=2)
        rows = over_four(rows, "seq", 1)
        other = across(rows, 4)
        rows = jnp.stack([jnp.where(half == 0, rows, other), jnp.where(half == 0, other, rows)], axis=1)
        rows = over_four(rows, "dp", 1).reshape(HEADS, 2, HEAD_DIM)
    with jax.named_scope("return"):
        got = across(front[:, 512:1024], 6)
        attended, query_grad = mover(unpack_front_kernel, "unpack_front", (ROWS, ROWS), mine, front, got)
        key_grad, value_grad = mover(unpack_kernel, "unpack", (ROWS, ROWS), along_z(kv_grad))
    return (attended[None], query_grad[None], key_grad[None], value_grad[None], rows[:, 0], rows[:, 1])


def solution(mesh):
    rows = P("dp", "seq", None)
    return jax.shard_map(
        body,
        mesh=mesh,
        in_specs=(rows, rows, rows, rows, P(), P(), P("dp", None, None, None), P("dp", None, None)),
        out_specs=(rows, rows, rows, rows, P(), P()),
        check_vma=False,
    )
```
